256 devices in a mesh: group: 32 (over z, y_hi, core), member: 8 (over y_lo, x).
Axes of the slice: x: 4, y: 4 (y_hi: 2, y_lo: 2; y = y_hi * 2 + y_lo), z: 8, core: 2. Of those that a mesh axis runs over, the one named last changes fastest.
Arguments:
- hidden_states: bfloat16 [32768, 4096], P(('group', 'member')), may hold values from -24 to 24
- queries: bfloat16 [32768, 2048], P(('group', 'member')), may hold values from -5 to 5
- local_keys: bfloat16 [32768, 2048], P(('group', 'member')), may hold values from -5 to 5
- local_values: bfloat16 [32768, 2048], P(('group', 'member')), may hold values from -6 to 6
- memory_keys: bfloat16 [16384, 2048], P(('group', 'member')), may hold values from -5 to 5
- memory_values: bfloat16 [16384, 2048], P(('group', 'member')), may hold values from -6 to 6
- grad_output: bfloat16 [32768, 2048], P(('group', 'member')), may hold values from -192 to 192
Outputs:
- grad_queries: bfloat16 [32768, 2048], P(('group', 'member'))
- grad_local_keys: bfloat16 [32768, 2048], P(('group', 'member'))
- grad_local_values: bfloat16 [32768, 2048], P(('group', 'member'))
- grad_memory_keys: bfloat16 [16384, 2048], P(('group', 'member'))
- grad_memory_values: bfloat16 [16384, 2048], P(('group', 'member'))
- grad_weight: float32 [4096, 2048], P(('group', 'member'))
The draws below stay inside these ranges and needn't reach their ends.
All inputs are finite; a program needn't handle non-finite values.
Results may differ from the reference program's by a relative error of at most 0.024.
Values may be sent and summed in bfloat16 or wider, within the bound.
No kernel may reach another device: no remote copies, remote signals or barrier semaphores. Data moves between devices by JAX's collectives and lax.ppermute only.
A program may use at most 128 MiB of HBM per device.

```python
import jax
import jax.numpy as jnp
from jax import lax

WIDTH = 4096
HEADS = 16
HEAD_DIM = 128
QUERY_LEN = 128
MEMORY_LEN = 64
INNER = 2048
GROUP_DOCS = 8
GROUPS = 32
DOCS = 256


def shared_signs(key):
    flips = jax.random.bernoulli(jax.random.fold_in(key, 97), 0.5, (INNER,))
    return jnp.where(flips, 1.0, -1.0).astype(jnp.float32)


def draw_queries(key, part):
    sign_row = shared_signs(key)
    key = jax.random.fold_in(key, 11)
    row_total = DOCS * QUERY_LEN
    values = jnp.clip(jax.random.normal(key, (row_total, INNER), jnp.float32) * sign_row[None, :], -5.0, 5.0)
    return values.astype(jnp.bfloat16)


def draw_local_keys(key, part):
    key = jax.random.fold_in(key, 23)
    row_total = DOCS * QUERY_LEN
    values = jnp.clip(jax.random.normal(key, (row_total, INNER), jnp.float32), -5.0, 5.0)
    return values.astype(jnp.bfloat16)


def draw_memory_keys(key, part):
    sign_row = shared_signs(key)
    key = jax.random.fold_in(key, 37)
    row_total = DOCS * MEMORY_LEN
    values = jnp.clip(jax.random.normal(key, (row_total, INNER), jnp.float32) * sign_row[None, :], -5.0, 5.0)
    return values.astype(jnp.bfloat16)


def spiked(array, own_key, source, target, shards_of, factor):
    owner, partner = [(jnp.arange(array.shape[axis_at]) // (array.shape[axis_at] // shards_of)).reshape([-1 if axis == axis_at else 1 for axis in range(array.ndim)]) for axis_at in (source, target)]
    chosen = jax.random.permutation(own_key, shards_of)[partner]
    strong = (owner == chosen) | (owner == (partner + shards_of // 2) % shards_of)
    return jnp.where(strong, factor * array, array)


def level_of(rng, shape, cuts, low, high):
    def one(dim, parts):
        steps = jax.random.uniform(jax.random.fold_in(jax.random.fold_in(rng, 6), dim), (parts,), jnp.float32, low / len(cuts), high / len(cuts))
        return jnp.repeat(jnp.exp(steps), shape[dim] // parts).reshape((-1,) + (1,) * (len(shape) - dim - 1))

    loudness = one(*cuts[0])
    for cut in cuts[1:]:
        loudness = loudness * one(*cut)
    return loudness


def gaussian(own_key, shape, scale, limit, cuts=(), dtype=jnp.bfloat16):
    gain = level_of(own_key, shape, cuts, -0.22, 0.18) if cuts else 1.0
    result = jax.random.normal(own_key, shape, jnp.float32) * scale * gain
    return jnp.minimum(jnp.maximum(result, -limit), limit).astype(dtype)


def gaussian_with(stream_key, shape, scale, reach, cuts, heavy, held_as=jnp.bfloat16):
    array = scale * jax.random.normal(stream_key, shape, jnp.float32)
    if cuts:
        array = array * level_of(stream_key, shape, cuts, -0.22, 0.18)
    return jnp.clip(spiked(array, jax.random.fold_in(stream_key, 3), *heavy), -reach, reach).astype(held_as)


def setup_inputs(seed: int = 0) -> dict:
    keys = jax.random.split(jax.random.key(seed), 8)
    return {
        "hidden_states": gaussian_with(keys[0], (DOCS * QUERY_LEN, WIDTH), 1.0, 24.0, ((0, 256),), (0, 1, 256, 6.0)),
        "queries": draw_queries(jax.random.fold_in(keys[7], 71), 0),
        "local_keys": draw_local_keys(jax.random.fold_in(keys[7], 71), 0),
        "local_values": gaussian(keys[3], (DOCS * QUERY_LEN, INNER), 1.0, 6.0, ((0, 256),)),
        "memory_keys": draw_memory_keys(jax.random.fold_in(keys[7], 71), 0),
        "memory_values": gaussian(keys[5], (DOCS * MEMORY_LEN, INNER), 1.0, 6.0, ((0, 256),)),
        "grad_output": gaussian(keys[6], (DOCS * QUERY_LEN, INNER), 32.0, 192.0, ((0, 256),)),
    }


def split_heads(matrix):
    return matrix.astype(jnp.float32).reshape(matrix.shape[0], HEADS, HEAD_DIM)


def rounded(values):
    return lax.optimization_barrier(values.astype(jnp.bfloat16)).astype(jnp.float32)


def document_backward(query_rows, key_rows, value_rows, grad_rows, group_keys, group_values):
    score_scale = HEAD_DIM ** -0.5
    row_count = query_rows.shape[0]
    inner_width = query_rows.shape[1]
    query_heads = split_heads(query_rows)
    grad_heads = split_heads(grad_rows)
    local_key_heads = split_heads(key_rows)
    local_value_heads = split_heads(value_rows)
    memory_key_heads = split_heads(group_keys)
    memory_value_heads = split_heads(group_values)
    positions = jnp.arange(row_count)
    visible = positions[:, None, None] <= positions[None, None, :]
    local_scores = jnp.where(visible, jnp.einsum("khd,qhd->khq", local_key_heads, query_heads) * score_scale, -jnp.inf)
    memory_scores = jnp.einsum("khd,qhd->khq", memory_key_heads, query_heads) * score_scale
    row_max = jnp.maximum(jnp.max(local_scores, axis=0), jnp.max(memory_scores, axis=0))
    local_exp = jnp.exp(local_scores - row_max)
    memory_exp = jnp.exp(memory_scores - row_max)
    denominator = jnp.sum(local_exp, axis=0) + jnp.sum(memory_exp, axis=0)
    local_prob = local_exp / denominator
    memory_prob = memory_exp / denominator
    local_prob_grad = jnp.einsum("khd,qhd->khq", local_value_heads, grad_heads)
    memory_prob_grad = jnp.einsum("khd,qhd->khq", memory_value_heads, grad_heads)
    delta_row = jnp.sum(local_prob * local_prob_grad, axis=0) + jnp.sum(memory_prob * memory_prob_grad, axis=0)
    local_dscore = rounded(local_prob * (local_prob_grad - delta_row))
    memory_dscore = rounded(memory_prob * (memory_prob_grad - delta_row))
    local_prob_low = rounded(local_prob)
    memory_prob_low = rounded(memory_prob)
    grad_query = score_scale * (jnp.einsum("khq,khd->qhd", local_dscore, local_key_heads) + jnp.einsum("khq,khd->qhd", memory_dscore, memory_key_heads))
    grad_queries = grad_query.reshape(row_count, inner_width).astype(jnp.bfloat16)
    grad_local_keys = (score_scale * jnp.einsum("khq,qhd->khd", local_dscore, query_heads)).reshape(row_count, inner_width).astype(jnp.bfloat16)
    grad_local_values = jnp.einsum("khq,qhd->khd", local_prob_low, grad_heads).reshape(row_count, inner_width).astype(jnp.bfloat16)
    key_terms = rounded(score_scale * jnp.einsum("khq,qhd->khd", memory_dscore, query_heads)).reshape(-1, inner_width)
    value_terms = rounded(jnp.einsum("khq,qhd->khd", memory_prob_low, grad_heads)).reshape(-1, inner_width)
    return grad_queries, grad_local_keys, grad_local_values, key_terms, value_terms


def reference(hidden_states, queries, local_keys, local_values, memory_keys, memory_values, grad_output):
    inner_width = queries.shape[1]

    def by_group(matrix, length):
        return matrix.reshape(GROUPS, GROUP_DOCS, length, matrix.shape[1])

    stacked = (by_group(hidden_states, QUERY_LEN), by_group(queries, QUERY_LEN), by_group(local_keys, QUERY_LEN),
               by_group(local_values, QUERY_LEN), by_group(grad_output, QUERY_LEN),
               by_group(memory_keys, MEMORY_LEN), by_group(memory_values, MEMORY_LEN))

    def group_step(weight_sum, items):
        hidden_group, query_group, key_group, value_group, grad_group, memory_key_group, memory_value_group = items
        group_keys = memory_key_group.reshape(GROUP_DOCS * MEMORY_LEN, inner_width)
        group_values = memory_value_group.reshape(GROUP_DOCS * MEMORY_LEN, inner_width)

        def one_document(pieces):
            return document_backward(pieces[0], pieces[1], pieces[2], pieces[3], group_keys, group_values)

        query_grads, local_key_grads, local_value_grads, key_terms, value_terms = lax.map(
            one_document, (query_group, key_group, value_group, grad_group))
        memory_key_grads = jnp.sum(key_terms, axis=0).astype(jnp.bfloat16)
        memory_value_grads = jnp.sum(value_terms, axis=0).astype(jnp.bfloat16)

        def add_document(running, pair):
            term = lax.dot_general(pair[0], pair[1], (((0,), (0,)), ((), ())), preferred_element_type=jnp.float32)
            return running + rounded(term), None

        weight_sum, _ = lax.scan(add_document, weight_sum, (hidden_group, query_grads))
        return weight_sum, (query_grads, local_key_grads, local_value_grads, memory_key_grads, memory_value_grads)

    weight_sum, outputs = lax.scan(group_step, jnp.zeros((WIDTH, inner_width), jnp.float32), stacked)
    grad_queries = outputs[0].reshape(-1, inner_width)
    grad_local_keys = outputs[1].reshape(-1, inner_width)
    grad_local_values = outputs[2].reshape(-1, inner_width)
    grad_memory_keys = outputs[3].reshape(-1, inner_width)
    grad_memory_values = outputs[4].reshape(-1, inner_width)
    grad_weight = weight_sum / (GROUPS * GROUP_DOCS)
    return (grad_queries, grad_local_keys, grad_local_values, grad_memory_keys, grad_memory_values, grad_weight)
```

```python
import jax
import jax.numpy as jnp
from jax import lax
from jax.experimental import pallas as pl
from jax.experimental.pallas import tpu as pltpu
from jax.sharding import PartitionSpec as P

HEAD_DIM = 128
DOCS = 8
ROWS = 128
MEM = 64
WIDTH = 4096
INNER = 2048
BATCHES = 2
SPAN = 2 * HEAD_DIM // BATCHES
AXES = ("group", "member")
LOW = jnp.bfloat16
FULL = jnp.float32


def coords(i):
    g, m = divmod(i, 8)
    return {"z": g // 4, "yh": (g // 2) % 2, "c": g % 2, "yl": m // 4, "x": m % 4}


def index_of(d):
    return (d["z"] * 4 + d["yh"] * 2 + d["c"]) * 8 + d["yl"] * 4 + d["x"]


def pairs(key, size, step):
    out = []
    for i in range(256):
        d = coords(i)
        d[key] = (d[key] + step) % size
        out.append((i, index_of(d)))
    return out


X_GROUPS = [[0, 1, 2, 3], [4, 5, 6, 7]]
Z_GROUPS = [[z * 4 + r for z in range(8)] for r in range(4)]
Y_GROUPS = [
    [index_of({"z": z, "yh": y // 2, "c": c, "yl": y % 2, "x": x}) for y in range(4)]
    for z in range(8)
    for c in range(2)
    for x in range(4)
]


def dot(left, right, left_dim, right_dim):
    return lax.dot_general(
        left, right, (((left_dim,), (right_dim,)), ((), ())), preferred_element_type=FULL
    )


def pack_kernel(q_ref, g_ref, k_ref, v_ref, mk_ref, mv_ref, *outs):
    for j, out in enumerate(outs):
        cols = slice(j * SPAN, (j + 1) * SPAN)
        for n, ref in enumerate((q_ref, g_ref, k_ref, v_ref)):
            out[0, n * ROWS : (n + 1) * ROWS, :] = ref[:, cols]
        out[0, 4 * ROWS : 4 * ROWS + MEM, :] = mk_ref[:, cols]
        out[0, 4 * ROWS + MEM :, :] = mv_ref[:, cols]


def pack(q, g, k, v, mk, mv):
    tall = pl.BlockSpec((ROWS, 256), lambda i: (0, i))
    short = pl.BlockSpec((MEM, 256), lambda i: (0, i))
    return pl.pallas_call(
        pack_kernel,
        grid=(DOCS,),
        in_specs=[tall] * 4 + [short] * 2,
        out_specs=[pl.BlockSpec((1, 640, SPAN), lambda i: (i, 0, 0))] * BATCHES,
        out_shape=[jax.ShapeDtypeStruct((DOCS, 640, SPAN), LOW)] * BATCHES,
        cost_estimate=pl.CostEstimate(flops=0, bytes_accessed=5 << 20, transcendentals=0),
        name="pack_heads",
    )(q, g, k, v, mk, mv)


def hidden_kernel(h_ref, out_ref, perm):
    @pl.when(pl.program_id(0) == 0)
    def _():
        src = lax.broadcasted_iota(jnp.int32, (1024, 1024), 0)
        dst = lax.broadcasted_iota(jnp.int32, (1024, 1024), 1)
        x, c, zl = dst >> 8, (dst >> 7) & 1, (dst >> 6) & 1
        yh, yl, i = (dst >> 5) & 1, (dst >> 4) & 1, dst & 15
        want = (zl << 9) | (yh << 8) | (c << 7) | (yl << 6) | (x << 4) | i
        perm[...] = jnp.where(src == want, 1.0, 0.0).astype(LOW)

    moved = jnp.dot(h_ref[...], perm[...], preferred_element_type=FULL).astype(LOW)
    for x in range(4):
        for c in range(2):
            lane = x * 256 + c * 128
            out_ref[x, c, :, :] = moved[:, lane : lane + 128]


def hidden_pieces(hidden):
    return pl.pallas_call(
        hidden_kernel,
        grid=(4,),
        in_specs=[pl.BlockSpec((ROWS, 1024), lambda t: (0, t))],
        out_specs=pl.BlockSpec((4, 2, ROWS, 128), lambda t: (0, 0, 0, t)),
        out_shape=jax.ShapeDtypeStruct((4, 2, ROWS, 512), LOW),
        scratch_shapes=[pltpu.VMEM((1024, 1024), LOW)],
        compiler_params=pltpu.CompilerParams(vmem_limit_bytes=32 << 20),
        cost_estimate=pl.CostEstimate(flops=1 << 30, bytes_accessed=2 << 20, transcendentals=0),
        name="pack_hidden",
    )(hidden)


def attention_kernel(doc_ref, mk_ref, mv_ref, out_ref, gq_ref, dk_acc, dv_acc):
    doc = pl.program_id(1)
    scale = HEAD_DIM**-0.5
    q = doc_ref[0, 0:ROWS, :]
    g = doc_ref[0, ROWS : 2 * ROWS, :]
    k = doc_ref[0, 2 * ROWS : 3 * ROWS, :]
    v = doc_ref[0, 3 * ROWS : 4 * ROWS, :]
    mk = mk_ref[...].reshape(DOCS * MEM, HEAD_DIM)
    mv = mv_ref[...].reshape(DOCS * MEM, HEAD_DIM)
    key_at = lax.broadcasted_iota(jnp.int32, (ROWS, ROWS), 0)
    query_at = lax.broadcasted_iota(jnp.int32, (ROWS, ROWS), 1)
    s_loc = jnp.where(key_at <= query_at, dot(k, q, 1, 1) * scale, -jnp.inf)
    s_mem = dot(mk, q, 1, 1) * scale
    dp_loc = dot(v, g, 1, 1)
    dp_mem = dot(mv, g, 1, 1)
    top = jnp.maximum(
        jnp.max(s_loc, axis=0, keepdims=True), jnp.max(s_mem, axis=0, keepdims=True)
    )
    e_loc = jnp.exp(s_loc - top)
    e_mem = jnp.exp(s_mem - top)
    total = jnp.sum(e_loc, axis=0, keepdims=True) + jnp.sum(e_mem, axis=0, keepdims=True)
    inverse = 1.0 / total
    p_loc = e_loc * inverse
    p_mem = e_mem * inverse
    delta = jnp.sum(p_loc * dp_loc, axis=0, keepdims=True) + jnp.sum(
        p_mem * dp_mem, axis=0, keepdims=True
    )
    ds_loc = (p_loc * (dp_loc - delta)).astype(LOW)
    ds_mem = (p_mem * (dp_mem - delta)).astype(LOW)
    gq = (scale * (dot(ds_loc, k, 0, 0) + dot(ds_mem, mk, 0, 0))).astype(LOW)
    gq_ref[doc] = gq
    out_ref[doc, 0:ROWS, :] = gq
    out_ref[doc, ROWS : 2 * ROWS, :] = (scale * dot(ds_loc, q, 1, 0)).astype(LOW)
    out_ref[doc, 2 * ROWS : 3 * ROWS, :] = dot(p_loc.astype(LOW), g, 1, 0).astype(LOW)
    dk = scale * dot(ds_mem, q, 1, 0)
    dv = dot(p_mem.astype(LOW), g, 1, 0)

    @pl.when(doc == 0)
    def _():
        dk_acc[...] = dk
        dv_acc[...] = dv

    @pl.when(doc > 0)
    def _():
        dk_acc[...] += dk
        dv_acc[...] += dv

    @pl.when(doc == DOCS - 1)
    def _():
        out_ref[:, 3 * ROWS : 3 * ROWS + MEM, :] = (
            dk_acc[...].reshape(DOCS, MEM, HEAD_DIM).astype(LOW)
        )
        out_ref[:, 3 * ROWS + MEM :, :] = dv_acc[...].reshape(DOCS, MEM, HEAD_DIM).astype(LOW)


def attention(received):
    return pl.pallas_call(
        attention_kernel,
        grid=(SPAN // HEAD_DIM, DOCS),
        in_specs=[
            pl.BlockSpec((1, 512, HEAD_DIM), lambda h, d: (d, 0, h)),
            pl.BlockSpec((DOCS, MEM, HEAD_DIM), lambda h, d: (0, 8, h)),
            pl.BlockSpec((DOCS, MEM, HEAD_DIM), lambda h, d: (0, 9, h)),
        ],
        out_specs=[
            pl.BlockSpec((DOCS, 512, HEAD_DIM), lambda h, d: (0, 0, h)),
            pl.BlockSpec((DOCS, ROWS, HEAD_DIM), lambda h, d: (0, 0, h)),
        ],
        out_shape=[
            jax.ShapeDtypeStruct((DOCS, 512, SPAN), LOW),
            jax.ShapeDtypeStruct((DOCS, ROWS, SPAN), LOW),
        ],
        scratch_shapes=[pltpu.VMEM((DOCS * MEM, HEAD_DIM), FULL)] * 2,
        compiler_params=pltpu.CompilerParams(vmem_limit_bytes=32 << 20),
        cost_estimate=pl.CostEstimate(
            flops=int(3.4e9) // BATCHES, bytes_accessed=(5 << 20) // BATCHES, transcendentals=1 << 20
        ),
        name="attention_backward",
    )(received, received, received)


def product_kernel(place, own_ref, other_ref, *refs):
    pieces, (send_ref, keep_ref) = refs[:-2], refs[-2:]
    yl = place[1]
    for n, piece in enumerate(pieces):
        cols = slice(n * SPAN, (n + 1) * SPAN)
        near = piece[pl.ds(pl.multiple_of(yl * 4, 4), 4)].reshape(512, SPAN)
        far = piece[pl.ds(pl.multiple_of(4 - yl * 4, 4), 4)].reshape(512, SPAN)
        part = dot(own_ref[...].reshape(512, 512), near, 0, 0)
        part = part + dot(other_ref[...].reshape(512, 512), far, 0, 0)

        @pl.when(pl.program_id(0) == 0)
        def _():
            send_ref[:, cols] = part.astype(LOW)

        @pl.when(pl.program_id(0) == 1)
        def _():
            keep_ref[:, cols] = part.astype(LOW)


def product(place, own, other, pieces):
    half = pl.BlockSpec((4, None, ROWS, 512), lambda i, s: (0, (1 - s[0]) * (1 - i) + s[0] * i, 0, 0))
    whole = pl.BlockSpec((DOCS, ROWS, SPAN), lambda i, s: (0, 0, 0))
    out = pl.BlockSpec((512, 4 * SPAN), lambda i, s: (0, 0))
    return pl.pallas_call(
        product_kernel,
        grid_spec=pltpu.PrefetchScalarGridSpec(
            num_scalar_prefetch=1,
            grid=(2,),
            in_specs=[half, half] + [whole] * 4,
            out_specs=[out, out],
        ),
        out_shape=[jax.ShapeDtypeStruct((512, 4 * SPAN), LOW)] * 2,
        compiler_params=pltpu.CompilerParams(vmem_limit_bytes=32 << 20),
        cost_estimate=pl.CostEstimate(
            flops=int(2.1e9) // BATCHES, bytes_accessed=6 << 20, transcendentals=0
        ),
        name="weight_product",
    )(place, own, other, *pieces)


def unpack_kernel(*refs):
    ins, outs = refs[:BATCHES], refs[BATCHES:]
    for j, ref in enumerate(ins):
        cols = slice(j * SPAN, (j + 1) * SPAN)
        for n in range(3):
            outs[n][:, cols] = ref[0, n * ROWS : (n + 1) * ROWS, :]
        outs[3][:, cols] = ref[0, 3 * ROWS : 3 * ROWS + MEM, :]
        outs[4][:, cols] = ref[0, 3 * ROWS + MEM :, :]


def unpack(returned):
    tall = pl.BlockSpec((ROWS, 256), lambda i: (0, i))
    short = pl.BlockSpec((MEM, 256), lambda i: (0, i))
    return pl.pallas_call(
        unpack_kernel,
        grid=(DOCS,),
        in_specs=[pl.BlockSpec((1, 512, SPAN), lambda i: (i, 0, 0))] * BATCHES,
        out_specs=[tall] * 3 + [short] * 2,
        out_shape=[jax.ShapeDtypeStruct((ROWS, INNER), LOW)] * 3
        + [jax.ShapeDtypeStruct((MEM, INNER), LOW)] * 2,
        cost_estimate=pl.CostEstimate(flops=0, bytes_accessed=4 << 20, transcendentals=0),
        name="unpack_heads",
    )(*returned)


def local(
    hidden_states, queries, local_keys, local_values, memory_keys, memory_values, grad_output
):
    core = lax.rem(lax.axis_index("group"), 2)
    member = lax.axis_index("member")
    yl, x = member // 4, lax.rem(member, 4)
    place = jnp.stack((core, yl)).astype(jnp.int32)

    sends = pack(queries, grad_output, local_keys, local_values, memory_keys, memory_values)
    hidden = hidden_pieces(hidden_states)
    arrived = [lax.all_to_all(s, "member", 0, 0, tiled=True) for s in sends]
    own = lax.all_to_all(hidden, "member", 0, 0, axis_index_groups=X_GROUPS, tiled=True)
    other = lax.ppermute(own, AXES, pairs("yl", 2, 1))

    returned = []
    summed = []
    for block in arrived:
        grads, gq = attention(block)
        returned.append(lax.all_to_all(grads, "member", 0, 0, tiled=True))
        pieces = [gq] + [lax.ppermute(gq, AXES, pairs("x", 4, k)) for k in (1, 2, 3)]
        send, keep = product(place, own, other, pieces)
        swapped = lax.ppermute(send, AXES, pairs("c", 2, 1))
        both = (keep.astype(FULL) + swapped.astype(FULL)).astype(LOW).reshape(8, 64, 4 * SPAN)
        along_z = lax.all_to_all(both, "group", 0, 0, axis_index_groups=Z_GROUPS, tiled=True)
        z_sum = jnp.sum(along_z.astype(FULL), axis=0).astype(LOW).reshape(4, 16, 4 * SPAN)
        along_y = lax.all_to_all(z_sum, AXES, 0, 0, axis_index_groups=Y_GROUPS, tiled=True)
        y_sum = along_y[:2].astype(FULL) + along_y[2:].astype(FULL)
        summed.append(y_sum.reshape(2, 16, 4, SPAN))
    weight = jnp.concatenate(summed, axis=3) * (1.0 / 256)
    order = lax.rem(x - jnp.arange(4) + 4, 4)
    weight = jnp.take(weight, order, axis=2)
    grad_weight = jnp.transpose(weight, (1, 0, 2, 3)).reshape(16, INNER)
    gq, glk, glv, gmk, gmv = unpack(returned)
    return gq, glk, glv, gmk, gmv, grad_weight


def solution(mesh):
    spec = P(("group", "member"), None)
    return jax.shard_map(
        local, mesh=mesh, in_specs=(spec,) * 7, out_specs=(spec,) * 6, check_vma=False
    )
```

```python
import jax
import jax.numpy as jnp
from jax import lax
from jax.experimental import pallas as pl
from jax.experimental.pallas import tpu as pltpu
from jax.sharding import PartitionSpec as P

HEAD_DIM = 128
DOCS = 8
ROWS = 128
MEM = 64
WIDTH = 4096
INNER = 2048
SPAN = 2 * HEAD_DIM
AXES = ("group", "member")
LOW = jnp.bfloat16
FULL = jnp.float32


def coords(i):
    g, m = divmod(i, 8)
    return {"z": g // 4, "yh": (g // 2) % 2, "c": g % 2, "yl": m // 4, "x": m % 4}


def index_of(d):
    return (d["z"] * 4 + d["yh"] * 2 + d["c"]) * 8 + d["yl"] * 4 + d["x"]


def pairs(key, size, step):
    out = []
    for i in range(256):
        d = coords(i)
        d[key] = (d[key] + step) % size
        out.append((i, index_of(d)))
    return out


ZY_GROUPS = [
    [
        index_of({"z": z, "yh": yh, "c": c, "yl": yl, "x": x})
        for z in range(8)
        for yh in range(2)
        for yl in range(2)
    ]
    for c in range(2)
    for x in range(4)
]
ANY = pl.BlockSpec(memory_space=pl.ANY)
VMEM = pl.BlockSpec(memory_space=pltpu.VMEM)
SMEM = pl.BlockSpec(memory_space=pltpu.SMEM)


def shift(array, key, size, step):
    return lax.ppermute(array, AXES, pairs(key, size, step))


def dot(left, right, left_dim, right_dim):
    return lax.dot_general(
        left, right, (((left_dim,), (right_dim,)), ((), ())), preferred_element_type=FULL
    )


def pack_kernel(q_ref, g_ref, k_ref, v_ref, mk_ref, mv_ref, out):
    for m in range(4):
        cols = slice(m * SPAN, (m + 1) * SPAN)
        for n, ref in enumerate((q_ref, g_ref, k_ref, v_ref)):
            out[m, n * ROWS : (n + 1) * ROWS, :] = ref[:, cols]
        out[m, 4 * ROWS : 4 * ROWS + MEM, :] = mk_ref[:, cols]
        out[m, 4 * ROWS + MEM :, :] = mv_ref[:, cols]


def pack(q, g, k, v, mk, mv):
    tall = pl.BlockSpec((ROWS, 4 * SPAN), lambda i: (0, i))
    short = pl.BlockSpec((MEM, 4 * SPAN), lambda i: (0, i))
    return pl.pallas_call(
        pack_kernel,
        grid=(2,),
        in_specs=[tall] * 4 + [short] * 2,
        out_specs=pl.BlockSpec((4, 640, SPAN), lambda i: (i, 0, 0)),
        out_shape=jax.ShapeDtypeStruct((DOCS, 640, SPAN), LOW),
        cost_estimate=pl.CostEstimate(flops=0, bytes_accessed=5 << 20, transcendentals=0),
        name="pack_heads",
    )(q, g, k, v, mk, mv)


def hidden_kernel(place, h_ref, _, *refs):
    outs, perm = refs[:4], refs[4]
    dst = lax.broadcasted_iota(jnp.int32, (1024, 1), 0)
    src = lax.broadcasted_iota(jnp.int32, (1024, 1024), 1)
    x, c, zl = ((dst >> 8) + place[3]) & 3, (dst >> 7) & 1, (dst >> 6) & 1
    yh, yl, i = (dst >> 5) & 1, (dst >> 4) & 1, dst & 15
    want = (zl << 9) | (yh << 8) | (c << 7) | (yl << 6) | (x << 4) | i
    perm[...] = jnp.where(src == want, 1.0, 0.0).astype(LOW)
    for t in range(4):
        moved = dot(perm[...], h_ref[:, t * 1024 : (t + 1) * 1024], 1, 1).astype(LOW)
        for k, out in enumerate(outs):
            for c in range(2):
                row = k * 256 + c * 128
                out[c, t * 128 : (t + 1) * 128, :] = moved[row : row + 128, :]


def hidden_pieces(place, hidden, after):
    return pl.pallas_call(
        hidden_kernel,
        in_specs=[SMEM, VMEM, ANY],
        out_specs=[VMEM] * 4,
        out_shape=[jax.ShapeDtypeStruct((2, 512, ROWS), LOW)] * 4,
        scratch_shapes=[pltpu.VMEM((1024, 1024), LOW)],
        compiler_params=pltpu.CompilerParams(vmem_limit_bytes=24 << 20),
        cost_estimate=pl.CostEstimate(flops=1 << 30, bytes_accessed=2 << 20, transcendentals=0),
        name="pack_hidden",
    )(place, hidden, after)


def gate_kernel(*refs):
    pass


def gate(arrays, after):
    count = len(arrays)
    return pl.pallas_call(
        gate_kernel,
        in_specs=[ANY] * (count + 1),
        out_specs=[ANY] * count,
        out_shape=[jax.ShapeDtypeStruct(a.shape, a.dtype) for a in arrays],
        input_output_aliases={n: n for n in range(count)},
        compiler_params=pltpu.CompilerParams(vmem_limit_bytes=1 << 20),
        name="gate",
    )(*arrays, after)


def attention_kernel(place, doc_ref, mk_ref, mv_ref, *refs):
    outs = list(refs[:4]) + [refs[4].at[n] for n in range(4)]
    gq_ref, dk_acc, dv_acc = refs[5:]
    me = place[2]
    scale = HEAD_DIM**-0.5
    mk = mk_ref[...].reshape(DOCS * MEM, HEAD_DIM)
    mv = mv_ref[...].reshape(DOCS * MEM, HEAD_DIM)
    key_at = lax.broadcasted_iota(jnp.int32, (ROWS, ROWS), 0)
    query_at = lax.broadcasted_iota(jnp.int32, (ROWS, ROWS), 1)
    visible = key_at <= query_at
    for step in range(DOCS // 2):
        docs = [me ^ (2 * step), me ^ (2 * step + 1)]
        q = [doc_ref[d, 0:ROWS, :] for d in docs]
        g = [doc_ref[d, ROWS : 2 * ROWS, :] for d in docs]
        k = [doc_ref[d, 2 * ROWS : 3 * ROWS, :] for d in docs]
        v = [doc_ref[d, 3 * ROWS : 4 * ROWS, :] for d in docs]
        both_q = jnp.concatenate(q, axis=0)
        both_g = jnp.concatenate(g, axis=0)
        s_loc = jnp.concatenate(
            [jnp.where(visible, dot(k[n], q[n], 1, 1) * scale, -jnp.inf) for n in range(2)],
            axis=1,
        )
        dp_loc = jnp.concatenate([dot(v[n], g[n], 1, 1) for n in range(2)], axis=1)
        s_mem = dot(mk, both_q, 1, 1) * scale
        dp_mem = dot(mv, both_g, 1, 1)
        top = jnp.maximum(
            jnp.max(s_loc, axis=0, keepdims=True), jnp.max(s_mem, axis=0, keepdims=True)
        )
        e_loc = jnp.exp(s_loc - top)
        e_mem = jnp.exp(s_mem - top)
        total = jnp.sum(e_loc, axis=0, keepdims=True) + jnp.sum(e_mem, axis=0, keepdims=True)
        inverse = 1.0 / total
        p_loc = e_loc * inverse
        p_mem = e_mem * inverse
        delta = jnp.sum(p_loc * dp_loc, axis=0, keepdims=True) + jnp.sum(
            p_mem * dp_mem, axis=0, keepdims=True
        )
        ds_loc = (p_loc * (dp_loc - delta)).astype(LOW)
        ds_mem = (p_mem * (dp_mem - delta)).astype(LOW)
        low_loc = p_loc.astype(LOW)
        gq_mem = dot(ds_mem, mk, 0, 0)
        for n in range(2):
            rows = slice(n * ROWS, (n + 1) * ROWS)
            mine = ds_loc[:, rows]
            gq = (scale * (dot(mine, k[n], 0, 0) + gq_mem[rows, :])).astype(LOW)
            gq_ref[docs[n]] = gq
            out = outs[2 * step + n]
            out[0:ROWS, :] = gq
            out[ROWS : 2 * ROWS, :] = (scale * dot(mine, q[n], 1, 0)).astype(LOW)
            out[2 * ROWS : 3 * ROWS, :] = dot(low_loc[:, rows], g[n], 1, 0).astype(LOW)
        dk = scale * dot(ds_mem, both_q, 1, 0)
        dv = dot(p_mem.astype(LOW), both_g, 1, 0)
        if step == 0:
            dk_acc[...] = dk.reshape(DOCS, MEM, HEAD_DIM)
            dv_acc[...] = dv.reshape(DOCS, MEM, HEAD_DIM)
        else:
            dk_acc[...] += dk.reshape(DOCS, MEM, HEAD_DIM)
            dv_acc[...] += dv.reshape(DOCS, MEM, HEAD_DIM)
    for n, out in enumerate(outs):
        out[3 * ROWS : 3 * ROWS + MEM, :] = dk_acc[me ^ n].astype(LOW)
        out[3 * ROWS + MEM :, :] = dv_acc[me ^ n].astype(LOW)


def attention(place, received):
    return pl.pallas_call(
        attention_kernel,
        grid_spec=pltpu.PrefetchScalarGridSpec(
            num_scalar_prefetch=1,
            grid=(2,),
            in_specs=[
                pl.BlockSpec((DOCS, 512, HEAD_DIM), lambda h, s: (0, 0, h)),
                pl.BlockSpec((DOCS, MEM, HEAD_DIM), lambda h, s: (0, 8, h)),
                pl.BlockSpec((DOCS, MEM, HEAD_DIM), lambda h, s: (0, 9, h)),
            ],
            out_specs=[pl.BlockSpec((512, HEAD_DIM), lambda h, s: (0, h))] * 4
            + [
                pl.BlockSpec((4, 512, HEAD_DIM), lambda h, s: (0, 0, h)),
                pl.BlockSpec((DOCS, ROWS, HEAD_DIM), lambda h, s: (0, 0, h)),
            ],
            scratch_shapes=[pltpu.VMEM((DOCS, MEM, HEAD_DIM), FULL)] * 2,
        ),
        out_shape=[jax.ShapeDtypeStruct((512, SPAN), LOW)] * 4
        + [
            jax.ShapeDtypeStruct((4, 512, SPAN), LOW),
            jax.ShapeDtypeStruct((DOCS, ROWS, SPAN), LOW),
        ],
        compiler_params=pltpu.CompilerParams(vmem_limit_bytes=24 << 20),
        cost_estimate=pl.CostEstimate(
            flops=int(8e9), bytes_accessed=5 << 20, transcendentals=2 << 20
        ),
        name="attention_backward",
    )(place, received, received, received)


def product_kernel(place, *refs):
    near, far, pieces, (give_ref, keep_ref) = refs[:4], refs[4:8], refs[8:12], refs[12:]
    yl, x = place[1], place[3]
    mine = [yl * 4 + ((x + 4 - k) & 3) for k in range(4)]
    docs = mine + [d ^ 4 for d in mine]
    for out, half in ((give_ref, 1 - place[0]), (keep_ref, place[0])):
        left = jnp.concatenate([ref[half] for ref in near + far], axis=1)
        for n, piece in enumerate(pieces):
            right = jnp.concatenate([piece[d] for d in docs], axis=0)
            out[:, n * SPAN : (n + 1) * SPAN] = dot(left, right, 1, 0).astype(LOW)


def product(place, near, far, pieces):
    return pl.pallas_call(
        product_kernel,
        in_specs=[SMEM] + [VMEM] * 12,
        out_specs=[VMEM] * 2,
        out_shape=[jax.ShapeDtypeStruct((512, 4 * SPAN), LOW)] * 2,
        compiler_params=pltpu.CompilerParams(vmem_limit_bytes=24 << 20),
        cost_estimate=pl.CostEstimate(flops=int(2.1e9), bytes_accessed=6 << 20, transcendentals=0),
        name="weight_product",
    )(place, *near, *far, *pieces)


def merge(keep, swapped, carried):
    count = len(carried)

    def kernel(a_ref, b_ref, *refs):
        refs[count][...] = (a_ref[...].astype(FULL) + b_ref[...].astype(FULL)).astype(LOW)

    return pl.pallas_call(
        kernel,
        in_specs=[VMEM] * 2 + [ANY] * count,
        out_specs=[VMEM] + [ANY] * count,
        out_shape=[jax.ShapeDtypeStruct(a.shape, LOW) for a in (keep, *carried)],
        input_output_aliases={2 + n: 1 + n for n in range(count)},
        compiler_params=pltpu.CompilerParams(vmem_limit_bytes=16 << 20),
        cost_estimate=pl.CostEstimate(flops=1 << 20, bytes_accessed=3 << 20, transcendentals=0),
        name="core_sum",
    )(keep, swapped, *carried)


def unpack_kernel(place, *refs):
    ins, outs = refs[:DOCS], refs[DOCS:]
    for n, ref in enumerate(ins):
        lane = pl.multiple_of((place[2] ^ n) * SPAN, SPAN)
        row = 0
        for out in outs:
            height = out.shape[0]
            out[:, pl.ds(lane, SPAN)] = ref[row : row + height, :]
            row += height


def unpack(place, returned):
    return pl.pallas_call(
        unpack_kernel,
        in_specs=[SMEM] + [VMEM] * DOCS,
        out_specs=[VMEM] * 5,
        out_shape=[jax.ShapeDtypeStruct((ROWS, INNER), LOW)] * 3
        + [jax.ShapeDtypeStruct((MEM, INNER), LOW)] * 2,
        compiler_params=pltpu.CompilerParams(vmem_limit_bytes=16 << 20),
        cost_estimate=pl.CostEstimate(flops=0, bytes_accessed=4 << 20, transcendentals=0),
        name="unpack_heads",
    )(place, *returned)


def finish_kernel(place, in_ref, out_ref):
    for y in range(2):
        total = in_ref[y].astype(FULL)
        for n in range(1, 16):
            total = total + in_ref[2 * n + y].astype(FULL)
        total = total * (1.0 / 256)
        for k in range(4):
            slot = (place[3] + 4 - k) & 3
            lane = pl.multiple_of(y * 1024 + slot * SPAN, SPAN)
            out_ref[:, pl.ds(lane, SPAN)] = total[:, k * SPAN : (k + 1) * SPAN]


def finish(place, along):
    return pl.pallas_call(
        finish_kernel,
        in_specs=[SMEM, VMEM],
        out_specs=VMEM,
        out_shape=jax.ShapeDtypeStruct((16, INNER), FULL),
        compiler_params=pltpu.CompilerParams(vmem_limit_bytes=16 << 20),
        cost_estimate=pl.CostEstimate(flops=1 << 20, bytes_accessed=1 << 20, transcendentals=0),
        name="weight_sum",
    )(place, along)


def local(
    hidden_states, queries, local_keys, local_values, memory_keys, memory_values, grad_output
):
    core = lax.rem(lax.axis_index("group"), 2)
    member = lax.axis_index("member")
    place = jnp.stack((core, member // 4, member, lax.rem(member, 4))).astype(jnp.int32)

    send = pack(queries, grad_output, local_keys, local_values, memory_keys, memory_values)
    arrived = lax.all_to_all(send, "member", 0, 0, tiled=True)
    hidden = gate(hidden_pieces(place, hidden_states, send), arrived)
    near = [hidden[0]] + [shift(hidden[k], "x", 4, k) for k in (1, 2, 3)]
    far = [shift(piece, "yl", 2, 1) for piece in near]
    *grads, grads_far, gq = attention(place, arrived)
    pieces = [gq] + [shift(gq, "x", 4, k) for k in (1, 2, 3)]
    grads_far = shift(grads_far, "yl", 2, 1)
    give, keep = product(place, near, far, pieces)
    swapped = shift(give, "c", 2, 1)
    both, *grads, grads_far = merge(keep, swapped, [*grads, grads_far])
    along = lax.all_to_all(
        both.reshape(32, 16, 4 * SPAN), AXES, 0, 0, axis_index_groups=ZY_GROUPS, tiled=True
    )
    returned = grads + [grads_far[k] for k in range(4)]
    returned = [
        lax.ppermute(piece, "member", [(i, i ^ (n & 3)) for i in range(DOCS)]) if n & 3 else piece
        for n, piece in enumerate(returned)
    ]
    gq_out, glk, glv, gmk, gmv = unpack(place, returned)
    grad_weight = finish(place, along)
    return gq_out, glk, glv, gmk, gmv, grad_weight


def solution(mesh):
    spec = P(("group", "member"), None)
    return jax.shard_map(
        local, mesh=mesh, in_specs=(spec,) * 7, out_specs=(spec,) * 6, check_vma=False
    )
```

```python
import jax
import jax.numpy as jnp
from jax import lax
from jax.experimental import pallas as pl
from jax.experimental.pallas import tpu as pltpu
from jax.sharding import PartitionSpec as P

HEAD_DIM = 128
DOCS = 8
ROWS = 128
MEM = 64
WIDTH = 4096
INNER = 2048
HALF = INNER // 2
PAIR = 2 * HEAD_DIM
AXES = ("group", "member")
LOW = jnp.bfloat16
FULL = jnp.float32


def coords(i):
    g, m = divmod(i, 8)
    return {"z": g // 4, "yh": (g // 2) % 2, "c": g % 2, "yl": m // 4, "x": m % 4}


def index_of(d):
    return (d["z"] * 4 + d["yh"] * 2 + d["c"]) * 8 + d["yl"] * 4 + d["x"]


def pairs(key, size, step):
    out = []
    for i in range(256):
        d = coords(i)
        d[key] = (d[key] + step) % size
        out.append((i, index_of(d)))
    return out


ZY_GROUPS = [
    [
        index_of({"z": z, "yh": yh, "c": c, "yl": yl, "x": x})
        for z in range(8)
        for yh in range(2)
        for yl in range(2)
    ]
    for c in range(2)
    for x in range(4)
]
ANY = pl.BlockSpec(memory_space=pl.ANY)
VMEM = pl.BlockSpec(memory_space=pltpu.VMEM)
SMEM = pl.BlockSpec(memory_space=pltpu.SMEM)


def shift(array, key, size, step):
    return lax.ppermute(array, AXES, pairs(key, size, step))


def dot(left, right, left_dim, right_dim):
    return lax.dot_general(
        left, right, (((left_dim,), (right_dim,)), ((), ())), preferred_element_type=FULL
    )


def pack_memory_kernel(place, mk_ref, mv_ref, near_ref, far_ref):
    for out, half in ((near_ref, place[1]), (far_ref, 1 - place[1])):
        cols = pl.ds(pl.multiple_of(half * HALF, HALF), HALF)
        out[0:MEM, :] = mk_ref[:, cols]
        out[MEM:, :] = mv_ref[:, cols]


def pack_memory(place, mk, mv):
    return pl.pallas_call(
        pack_memory_kernel,
        in_specs=[SMEM, VMEM, VMEM],
        out_specs=[VMEM] * 2,
        out_shape=[jax.ShapeDtypeStruct((2 * MEM, HALF), LOW)] * 2,
        cost_estimate=pl.CostEstimate(flops=0, bytes_accessed=1 << 20, transcendentals=0),
        name="pack_memory",
    )(place, mk, mv)


def pack_queries_kernel(place, q_ref, g_ref, k_ref, v_ref, *rest):
    out = rest[-1]
    for n, ref in enumerate((q_ref, g_ref, k_ref, v_ref)):
        out[n * ROWS : (n + 1) * ROWS, :] = ref[...]


def pack_queries(place, q, g, k, v, after):
    tall = pl.BlockSpec((ROWS, HALF), lambda i, s: (0, 1 - s[1]))
    return pl.pallas_call(
        pack_queries_kernel,
        grid_spec=pltpu.PrefetchScalarGridSpec(
            num_scalar_prefetch=1,
            grid=(1,),
            in_specs=[tall] * 4 + [ANY] * len(after),
            out_specs=pl.BlockSpec((4 * ROWS, HALF), lambda i, s: (0, 0)),
        ),
        out_shape=jax.ShapeDtypeStruct((4 * ROWS, HALF), LOW),
        cost_estimate=pl.CostEstimate(flops=0, bytes_accessed=2 << 20, transcendentals=0),
        name="pack_queries",
    )(place, q, g, k, v, *after)


def hidden_kernel(place, h_ref, *refs):
    outs, perm = refs[-5:-1], refs[-1]
    dst = lax.broadcasted_iota(jnp.int32, (1024, 1), 0)
    src = lax.broadcasted_iota(jnp.int32, (1024, 1024), 1)
    x, c, zl = ((dst >> 8) + place[3]) & 3, (dst >> 7) & 1, (dst >> 6) & 1
    yh, yl, i = (dst >> 5) & 1, (dst >> 4) & 1, dst & 15
    want = (zl << 9) | (yh << 8) | (c << 7) | (yl << 6) | (x << 4) | i
    perm[...] = jnp.where(src == want, 1.0, 0.0).astype(LOW)
    for t in range(4):
        moved = dot(perm[...], h_ref[:, t * 1024 : (t + 1) * 1024], 1, 1).astype(LOW)
        for k, out in enumerate(outs):
            for c in range(2):
                row = k * 256 + c * 128
                out[c, t * 128 : (t + 1) * 128, :] = moved[row : row + 128, :]


def hidden_pieces(place, hidden, after):
    return pl.pallas_call(
        hidden_kernel,
        in_specs=[SMEM, VMEM] + [ANY] * len(after),
        out_specs=[VMEM] * 4,
        out_shape=[jax.ShapeDtypeStruct((2, 512, ROWS), LOW)] * 4,
        scratch_shapes=[pltpu.VMEM((1024, 1024), LOW)],
        compiler_params=pltpu.CompilerParams(vmem_limit_bytes=24 << 20),
        cost_estimate=pl.CostEstimate(flops=1 << 30, bytes_accessed=2 << 20, transcendentals=0),
        name="pack_hidden",
    )(place, hidden, *after)


def gate_kernel(*refs):
    pass


def gate(arrays, after):
    count = len(arrays)
    return pl.pallas_call(
        gate_kernel,
        in_specs=[ANY] * (count + len(after)),
        out_specs=[ANY] * count,
        out_shape=[jax.ShapeDtypeStruct(a.shape, a.dtype) for a in arrays],
        input_output_aliases={n: n for n in range(count)},
        compiler_params=pltpu.CompilerParams(vmem_limit_bytes=1 << 20),
        name="gate",
    )(*arrays, *after)


def attention_kernel(place, q_ref, g_ref, k_ref, v_ref, far_ref, *refs):
    memory = refs[:4]
    gq_ref, local_ref, first_ref, back_ref = refs[4:8]
    term_refs = refs[8:]
    scale = HEAD_DIM**-0.5
    key_at = lax.broadcasted_iota(jnp.int32, (ROWS, ROWS), 0)
    query_at = lax.broadcasted_iota(jnp.int32, (ROWS, ROWS), 1)
    visible = key_at <= query_at
    for head in range(2):
        cols = slice(head * HEAD_DIM, (head + 1) * HEAD_DIM)
        q, g, k, v = [
            [ref[:, cols], far_ref[n * ROWS : (n + 1) * ROWS, cols]]
            for n, ref in enumerate((q_ref, g_ref, k_ref, v_ref))
        ]
        mk = jnp.concatenate([ref[n, 0:MEM, cols] for n in range(2) for ref in memory], axis=0)
        mv = jnp.concatenate([ref[n, MEM:, cols] for n in range(2) for ref in memory], axis=0)
        both_q = jnp.concatenate(q, axis=0)
        both_g = jnp.concatenate(g, axis=0)
        s_loc = jnp.concatenate(
            [jnp.where(visible, dot(k[n], q[n], 1, 1) * scale, -jnp.inf) for n in range(2)],
            axis=1,
        )
        dp_loc = jnp.concatenate([dot(v[n], g[n], 1, 1) for n in range(2)], axis=1)
        s_mem = dot(mk, both_q, 1, 1) * scale
        dp_mem = dot(mv, both_g, 1, 1)
        top = jnp.maximum(
            jnp.max(s_loc, axis=0, keepdims=True), jnp.max(s_mem, axis=0, keepdims=True)
        )
        e_loc = jnp.exp(s_loc - top)
        e_mem = jnp.exp(s_mem - top)
        total = jnp.sum(e_loc, axis=0, keepdims=True) + jnp.sum(e_mem, axis=0, keepdims=True)
        inverse = 1.0 / total
        p_loc = e_loc * inverse
        p_mem = e_mem * inverse
        delta = jnp.sum(p_loc * dp_loc, axis=0, keepdims=True) + jnp.sum(
            p_mem * dp_mem, axis=0, keepdims=True
        )
        ds_loc = (p_loc * (dp_loc - delta)).astype(LOW)
        ds_mem = (p_mem * (dp_mem - delta)).astype(LOW)
        low_loc = p_loc.astype(LOW)
        gq_mem = dot(ds_mem, mk, 0, 0)
        gq, glk, glv = [], [], []
        for n in range(2):
            rows = slice(n * ROWS, (n + 1) * ROWS)
            mine = ds_loc[:, rows]
            gq.append((scale * (dot(mine, k[n], 0, 0) + gq_mem[rows, :])).astype(LOW))
            glk.append((scale * dot(mine, q[n], 1, 0)).astype(LOW))
            glv.append(dot(low_loc[:, rows], g[n], 1, 0).astype(LOW))
        gq_ref[0:ROWS, cols] = gq[0]
        gq_ref[ROWS:, cols] = gq[1]
        local_ref[0:ROWS, cols] = glk[0]
        local_ref[ROWS:, cols] = glv[0]
        first_ref[:, cols] = gq[1]
        back_ref[0:ROWS, cols] = glk[1]
        back_ref[ROWS:, cols] = glv[1]
        dk = (scale * dot(ds_mem, both_q, 1, 0)).astype(LOW)
        dv = dot(p_mem.astype(LOW), both_g, 1, 0).astype(LOW)
        for n in range(8):
            rows = slice(n * MEM, (n + 1) * MEM)
            term_refs[n][0:MEM, cols] = dk[rows, :]
            term_refs[n][MEM:, cols] = dv[rows, :]


def attention(place, q, g, k, v, far, memory):
    def rows(count):
        return pl.BlockSpec((count, PAIR), lambda h, s: (0, h))

    mine = pl.BlockSpec((ROWS, PAIR), lambda h, s: (0, 4 * s[1] + h))
    whole = pl.BlockSpec((2, 2 * MEM, PAIR), lambda h, s: (0, 0, h))
    shapes = [(2 * ROWS, HALF), (2 * ROWS, HALF), (ROWS, HALF), (2 * ROWS, HALF)]
    shapes += [(2 * MEM, HALF)] * 8
    return pl.pallas_call(
        attention_kernel,
        grid_spec=pltpu.PrefetchScalarGridSpec(
            num_scalar_prefetch=1,
            grid=(4,),
            in_specs=[mine] * 4 + [rows(4 * ROWS)] + [whole] * 4,
            out_specs=[rows(shape[0]) for shape in shapes],
        ),
        out_shape=[jax.ShapeDtypeStruct(shape, LOW) for shape in shapes],
        compiler_params=pltpu.CompilerParams(vmem_limit_bytes=24 << 20),
        cost_estimate=pl.CostEstimate(
            flops=int(8e9), bytes_accessed=5 << 20, transcendentals=2 << 20
        ),
        name="attention_backward",
    )(place, q, g, k, v, far, *memory)


def product_half(place, half, out, refs):
    first, rest, pieces = refs[:4], refs[4:6], refs[6:10]
    left = jnp.concatenate(
        [ref[half] for ref in first] + [rest[0][half]] + [rest[1][k, half] for k in range(3)],
        axis=1,
    )
    for n in range(4):
        cols = slice(n * PAIR, (n + 1) * PAIR)
        right = jnp.concatenate(
            [p[0:ROWS, cols] for p in pieces] + [p[ROWS:, cols] for p in pieces], axis=0
        )
        out[:, cols] = dot(left, right, 1, 0).astype(LOW)


def give_kernel(place, *refs):
    product_half(place, 1 - place[0], refs[17], refs)


def keep_kernel(place, *refs):
    product_half(place, place[0], refs[11], refs)


def product_give(place, sources, carried, after):
    return pl.pallas_call(
        give_kernel,
        in_specs=[SMEM] + [VMEM] * 10 + [ANY] * 7,
        out_specs=[VMEM] + [ANY] * 6,
        out_shape=[jax.ShapeDtypeStruct((512, HALF), LOW)]
        + [jax.ShapeDtypeStruct(a.shape, LOW) for a in carried],
        input_output_aliases={11 + n: 1 + n for n in range(6)},
        compiler_params=pltpu.CompilerParams(vmem_limit_bytes=24 << 20),
        cost_estimate=pl.CostEstimate(flops=int(1e9), bytes_accessed=4 << 20, transcendentals=0),
        name="product_give",
    )(place, *sources, *carried, after)


def product_keep(place, sources, after):
    return pl.pallas_call(
        keep_kernel,
        in_specs=[SMEM] + [VMEM] * 10 + [ANY],
        out_specs=VMEM,
        out_shape=jax.ShapeDtypeStruct((512, HALF), LOW),
        compiler_params=pltpu.CompilerParams(vmem_limit_bytes=24 << 20),
        cost_estimate=pl.CostEstimate(flops=int(2e9), bytes_accessed=4 << 20, transcendentals=0),
        name="product_keep",
    )(place, *sources, after)


def merge_kernel(a_ref, b_ref, out_ref):
    out_ref[...] = (a_ref[...].astype(FULL) + b_ref[...].astype(FULL)).astype(LOW)


def merge(keep, swapped):
    return pl.pallas_call(
        merge_kernel,
        in_specs=[VMEM] * 2,
        out_specs=VMEM,
        out_shape=jax.ShapeDtypeStruct(keep.shape, LOW),
        compiler_params=pltpu.CompilerParams(vmem_limit_bytes=16 << 20),
        cost_estimate=pl.CostEstimate(flops=1 << 20, bytes_accessed=3 << 20, transcendentals=0),
        name="core_sum",
    )(keep, swapped)


def join_kernel(a_ref, b_ref, out_ref):
    out_ref[0] = a_ref[...]
    out_ref[1] = b_ref[...]


def join(a, b):
    return pl.pallas_call(
        join_kernel,
        in_specs=[VMEM] * 2,
        out_specs=VMEM,
        out_shape=jax.ShapeDtypeStruct((2, *a.shape), LOW),
        compiler_params=pltpu.CompilerParams(vmem_limit_bytes=8 << 20),
        cost_estimate=pl.CostEstimate(flops=0, bytes_accessed=1 << 20, transcendentals=0),
        name="join_memory",
    )(a, b)


def stack_kernel(*refs):
    for n in range(3):
        refs[-1][n] = refs[n][...]


def stack(arrays, after):
    return pl.pallas_call(
        stack_kernel,
        in_specs=[VMEM] * 3 + [ANY] * len(after),
        out_specs=VMEM,
        out_shape=jax.ShapeDtypeStruct((3, *arrays[0].shape), LOW),
        compiler_params=pltpu.CompilerParams(vmem_limit_bytes=16 << 20),
        cost_estimate=pl.CostEstimate(flops=0, bytes_accessed=2 << 20, transcendentals=0),
        name="stack_hidden",
    )(*arrays, *after)


def total_of(refs):
    total = refs[0][...].astype(FULL)
    for ref in refs[1:]:
        total = total + ref[...].astype(FULL)
    return total.astype(LOW)


def terms_kernel(*refs):
    refs[4][...] = total_of(refs[:4])


def sum_terms(terms):
    return pl.pallas_call(
        terms_kernel,
        in_specs=[VMEM] * 4,
        out_specs=VMEM,
        out_shape=jax.ShapeDtypeStruct((2 * MEM, HALF), LOW),
        compiler_params=pltpu.CompilerParams(vmem_limit_bytes=16 << 20),
        cost_estimate=pl.CostEstimate(flops=1 << 20, bytes_accessed=2 << 20, transcendentals=0),
        name="memory_sum",
    )(*terms)


def unpack_kernel(place, gq_ref, local_ref, first_ref, back_ref, got_ref, *refs):
    terms, outs = refs[:4], refs[4:]
    mine = pl.ds(pl.multiple_of(place[1] * HALF, HALF), HALF)
    theirs = pl.ds(pl.multiple_of((1 - place[1]) * HALF, HALF), HALF)
    outs[0][:, mine] = gq_ref[0:ROWS, :]
    outs[1][:, mine] = local_ref[0:ROWS, :]
    outs[2][:, mine] = local_ref[ROWS:, :]
    outs[0][:, theirs] = first_ref[...]
    outs[1][:, theirs] = back_ref[0:ROWS, :]
    outs[2][:, theirs] = back_ref[ROWS:, :]
    for value, cols in ((total_of(terms), mine), (got_ref[...], theirs)):
        outs[3][:, cols] = value[0:MEM, :]
        outs[4][:, cols] = value[MEM:, :]


def unpack(place, gq, local_grads, first, back, got, terms):
    return pl.pallas_call(
        unpack_kernel,
        in_specs=[SMEM] + [VMEM] * 9,
        out_specs=[VMEM] * 5,
        out_shape=[jax.ShapeDtypeStruct((ROWS, INNER), LOW)] * 3
        + [jax.ShapeDtypeStruct((MEM, INNER), LOW)] * 2,
        compiler_params=pltpu.CompilerParams(vmem_limit_bytes=16 << 20),
        cost_estimate=pl.CostEstimate(flops=0, bytes_accessed=4 << 20, transcendentals=0),
        name="unpack_heads",
    )(place, gq, local_grads, first, back, got, *terms)


def finish_kernel(in_ref, out_ref):
    for y in range(2):
        total = in_ref[y].astype(FULL)
        for n in range(1, 16):
            total = total + in_ref[2 * n + y].astype(FULL)
        out_ref[:, y * HALF : (y + 1) * HALF] = total * (1.0 / 256)


def finish(along):
    return pl.pallas_call(
        finish_kernel,
        in_specs=[VMEM],
        out_specs=VMEM,
        out_shape=jax.ShapeDtypeStruct((16, INNER), FULL),
        compiler_params=pltpu.CompilerParams(vmem_limit_bytes=16 << 20),
        cost_estimate=pl.CostEstimate(flops=1 << 20, bytes_accessed=1 << 20, transcendentals=0),
        name="weight_sum",
    )(along)


def local(
    hidden_states, queries, local_keys, local_values, memory_keys, memory_values, grad_output
):
    core = lax.rem(lax.axis_index("group"), 2)
    member = lax.axis_index("member")
    place = jnp.stack((core, member // 4, member, lax.rem(member, 4))).astype(jnp.int32)

    own_memory, give_memory = pack_memory(place, memory_keys, memory_values)
    other_memory = shift(give_memory, "yl", 2, 1)
    give_queries = pack_queries(
        place, queries, grad_output, local_keys, local_values, [own_memory]
    )
    joined = join(own_memory, other_memory)
    memory = [joined] + [shift(joined, "x", 4, k) for k in (1, 2, 3)]
    (give_queries,) = gate([give_queries], [joined])
    far_queries = shift(give_queries, "yl", 2, 1)

    hidden = hidden_pieces(place, hidden_states, [give_queries, joined])
    hidden = gate(hidden, memory[2:])
    near = [hidden[0]] + [shift(hidden[k], "x", 4, k) for k in (1, 2, 3)]

    gq, local_grads, first, back, *terms = attention(
        place, queries, grad_output, local_keys, local_values, far_queries, memory
    )
    pieces = [gq] + [shift(gq, "x", 4, k) for k in (1, 2, 3)]
    far = [shift(near[0], "yl", 2, 1)]
    far.append(shift(stack(near[1:], [gq, far[0]]), "yl", 2, 1))
    back = shift(back, "yl", 2, 1)
    first = shift(first, "yl", 2, 1)
    sources = near + far + pieces
    give, *moving = product_give(place, sources, terms[1:4] + terms[5:], first)
    keep = product_keep(place, sources, give)
    swapped = shift(give, "c", 2, 1)
    both = merge(keep, swapped)
    along = lax.all_to_all(
        both.reshape(32, 16, HALF), AXES, 0, 0, axis_index_groups=ZY_GROUPS, tiled=True
    )
    others = [terms[4]] + [shift(moving[2 + k], "x", 4, 4 - k) for k in (1, 2, 3)]
    got_sum = shift(sum_terms(others), "yl", 2, 1)
    nears = [terms[0]] + [shift(moving[k - 1], "x", 4, 4 - k) for k in (1, 2, 3)]
    gq_out, glk, glv, gmk, gmv = unpack(
        place, gq, local_grads, first, back, got_sum, nears
    )
    grad_weight = finish(along)
    return gq_out, glk, glv, gmk, gmv, grad_weight


def solution(mesh):
    spec = P(("group", "member"), None)
    return jax.shard_map(
        local, mesh=mesh, in_specs=(spec,) * 7, out_specs=(spec,) * 6, check_vma=False
    )
```

```python
import jax
import jax.numpy as jnp
from jax import lax
from jax.experimental import pallas as pl
from jax.experimental.pallas import tpu as pltpu
from jax.sharding import PartitionSpec as P

HEAD_DIM = 128
DOCS = 8
ROWS = 128
MEM = 64
WIDTH = 4096
INNER = 2048
HALF = INNER // 2
PAIR = 2 * HEAD_DIM
AXES = ("group", "member")
LOW = jnp.bfloat16
FULL = jnp.float32


def coords(i):
    g, m = divmod(i, 8)
    return {"z": g // 4, "yh": (g // 2) % 2, "c": g % 2, "yl": m // 4, "x": m % 4}


def index_of(d):
    return (d["z"] * 4 + d["yh"] * 2 + d["c"]) * 8 + d["yl"] * 4 + d["x"]


def pairs(key, size, step):
    out = []
    for i in range(256):
        d = coords(i)
        d[key] = (d[key] + step) % size
        out.append((i, index_of(d)))
    return out


ZY_GROUPS = [
    [
        index_of({"z": z, "yh": yh, "c": c, "yl": yl, "x": x})
        for z in range(8)
        for yh in range(2)
        for yl in range(2)
    ]
    for c in range(2)
    for x in range(4)
]
ANY = pl.BlockSpec(memory_space=pl.ANY)
VMEM = pl.BlockSpec(memory_space=pltpu.VMEM)
SMEM = pl.BlockSpec(memory_space=pltpu.SMEM)


def shift(array, key, size, step):
    return lax.ppermute(array, AXES, pairs(key, size, step))


def dot(left, right, left_dim, right_dim):
    return lax.dot_general(
        left, right, (((left_dim,), (right_dim,)), ((), ())), preferred_element_type=FULL
    )


def pack_memory_kernel(mk_ref, mv_ref, near_ref, far_ref):
    yl = lax.axis_index("member") // 4
    for out, half in ((near_ref, yl), (far_ref, 1 - yl)):
        cols = pl.ds(pl.multiple_of(half * HALF, HALF), HALF)
        out[0:MEM, :] = mk_ref[:, cols]
        out[MEM:, :] = mv_ref[:, cols]


def pack_memory(mk, mv):
    return pl.pallas_call(
        pack_memory_kernel,
        in_specs=[VMEM, VMEM],
        out_specs=[VMEM] * 2,
        out_shape=[jax.ShapeDtypeStruct((2 * MEM, HALF), LOW)] * 2,
        cost_estimate=pl.CostEstimate(flops=0, bytes_accessed=1 << 20, transcendentals=0),
        name="pack_memory",
    )(mk, mv)


def pack_queries_kernel(place, q_ref, g_ref, k_ref, v_ref, *rest):
    out = rest[-1]
    for n, ref in enumerate((q_ref, g_ref, k_ref, v_ref)):
        out[n * ROWS : (n + 1) * ROWS, :] = ref[...]


def pack_queries(place, q, g, k, v, after):
    tall = pl.BlockSpec((ROWS, HALF), lambda i, s: (0, 1 - s[1]))
    return pl.pallas_call(
        pack_queries_kernel,
        grid_spec=pltpu.PrefetchScalarGridSpec(
            num_scalar_prefetch=1,
            grid=(1,),
            in_specs=[tall] * 4 + [ANY] * len(after),
            out_specs=pl.BlockSpec((4 * ROWS, HALF), lambda i, s: (0, 0)),
        ),
        out_shape=jax.ShapeDtypeStruct((4 * ROWS, HALF), LOW),
        cost_estimate=pl.CostEstimate(flops=0, bytes_accessed=2 << 20, transcendentals=0),
        name="pack_queries",
    )(place, q, g, k, v, *after)


def hidden_kernel(place, h_ref, *refs):
    outs, perm = refs[-5:-1], refs[-1]
    dst = lax.broadcasted_iota(jnp.int32, (1024, 1), 0)
    src = lax.broadcasted_iota(jnp.int32, (1024, 1024), 1)
    x, c, zl = ((dst >> 8) + place[3]) & 3, (dst >> 7) & 1, (dst >> 6) & 1
    yh, yl, i = (dst >> 5) & 1, (dst >> 4) & 1, dst & 15
    want = (zl << 9) | (yh << 8) | (c << 7) | (yl << 6) | (x << 4) | i
    perm[...] = jnp.where(src == want, 1.0, 0.0).astype(LOW)
    for t in range(4):
        moved = dot(perm[...], h_ref[:, t * 1024 : (t + 1) * 1024], 1, 1).astype(LOW)
        for k, out in enumerate(outs):
            for c in range(2):
                row = k * 256 + c * 128
                out[c, t * 128 : (t + 1) * 128, :] = moved[row : row + 128, :]


def hidden_pieces(place, hidden, after):
    return pl.pallas_call(
        hidden_kernel,
        in_specs=[SMEM, VMEM] + [ANY] * len(after),
        out_specs=[VMEM] * 4,
        out_shape=[jax.ShapeDtypeStruct((2, 512, ROWS), LOW)] * 4,
        scratch_shapes=[pltpu.VMEM((1024, 1024), LOW)],
        compiler_params=pltpu.CompilerParams(vmem_limit_bytes=24 << 20),
        cost_estimate=pl.CostEstimate(flops=1 << 30, bytes_accessed=2 << 20, transcendentals=0),
        name="pack_hidden",
    )(place, hidden, *after)


def gate_kernel(*refs):
    pass


def gate(arrays, after):
    count = len(arrays)
    return pl.pallas_call(
        gate_kernel,
        in_specs=[ANY] * (count + len(after)),
        out_specs=[ANY] * count,
        out_shape=[jax.ShapeDtypeStruct(a.shape, a.dtype) for a in arrays],
        input_output_aliases={n: n for n in range(count)},
        compiler_params=pltpu.CompilerParams(vmem_limit_bytes=1 << 20),
        name="gate",
    )(*arrays, *after)


def attention_kernel(place, q_ref, g_ref, k_ref, v_ref, far_ref, *refs):
    memory = refs[:4]
    gq_ref, local_ref, first_ref, back_ref = refs[4:8]
    term_refs = refs[8:]
    scale = HEAD_DIM**-0.5
    key_at = lax.broadcasted_iota(jnp.int32, (ROWS, ROWS), 0)
    query_at = lax.broadcasted_iota(jnp.int32, (ROWS, ROWS), 1)
    visible = key_at <= query_at
    def one_head(head):
        cols = pl.ds(pl.multiple_of(head * HEAD_DIM, HEAD_DIM), HEAD_DIM)
        mine_cols = pl.ds(pl.multiple_of(place[1] * HALF + head * HEAD_DIM, HEAD_DIM), HEAD_DIM)
        q, g, k, v = [
            [ref[:, mine_cols], far_ref[n * ROWS : (n + 1) * ROWS, cols]]
            for n, ref in enumerate((q_ref, g_ref, k_ref, v_ref))
        ]
        mk = jnp.concatenate([ref[n, 0:MEM, cols] for n in range(2) for ref in memory], axis=0)
        mv = jnp.concatenate([ref[n, MEM:, cols] for n in range(2) for ref in memory], axis=0)
        both_q = jnp.concatenate(q, axis=0)
        both_g = jnp.concatenate(g, axis=0)
        s_loc = jnp.concatenate(
            [jnp.where(visible, dot(k[n], q[n], 1, 1) * scale, -jnp.inf) for n in range(2)],
            axis=1,
        )
        dp_loc = jnp.concatenate([dot(v[n], g[n], 1, 1) for n in range(2)], axis=1)
        s_mem = dot(mk, both_q, 1, 1) * scale
        dp_mem = dot(mv, both_g, 1, 1)
        top = jnp.maximum(
            jnp.max(s_loc, axis=0, keepdims=True), jnp.max(s_mem, axis=0, keepdims=True)
        )
        e_loc = jnp.exp(s_loc - top)
        e_mem = jnp.exp(s_mem - top)
        total = jnp.sum(e_loc, axis=0, keepdims=True) + jnp.sum(e_mem, axis=0, keepdims=True)
        inverse = 1.0 / total
        p_loc = e_loc * inverse
        p_mem = e_mem * inverse
        delta = jnp.sum(p_loc * dp_loc, axis=0, keepdims=True) + jnp.sum(
            p_mem * dp_mem, axis=0, keepdims=True
        )
        ds_loc = (p_loc * (dp_loc - delta)).astype(LOW)
        ds_mem = (p_mem * (dp_mem - delta)).astype(LOW)
        low_loc = p_loc.astype(LOW)
        gq_mem = dot(ds_mem, mk, 0, 0)
        gq, glk, glv = [], [], []
        for n in range(2):
            rows = slice(n * ROWS, (n + 1) * ROWS)
            mine = ds_loc[:, rows]
            gq.append((scale * (dot(mine, k[n], 0, 0) + gq_mem[rows, :])).astype(LOW))
            glk.append((scale * dot(mine, q[n], 1, 0)).astype(LOW))
            glv.append(dot(low_loc[:, rows], g[n], 1, 0).astype(LOW))
        gq_ref[0:ROWS, cols] = gq[0]
        gq_ref[ROWS:, cols] = gq[1]
        local_ref[0:ROWS, cols] = glk[0]
        local_ref[ROWS:, cols] = glv[0]
        first_ref[:, cols] = gq[1]
        back_ref[0:ROWS, cols] = glk[1]
        back_ref[ROWS:, cols] = glv[1]
        dk = (scale * dot(ds_mem, both_q, 1, 0)).astype(LOW)
        dv = dot(p_mem.astype(LOW), both_g, 1, 0).astype(LOW)
        for n in range(8):
            rows = slice(n * MEM, (n + 1) * MEM)
            term_refs[n][0:MEM, cols] = dk[rows, :]
            term_refs[n][MEM:, cols] = dv[rows, :]

    def two_heads(step, carry):
        one_head(2 * step)
        one_head(2 * step + 1)
        return carry

    lax.fori_loop(0, 4, two_heads, 0)


def attention(place, q, g, k, v, far, memory):
    shapes = [(2 * ROWS, HALF), (2 * ROWS, HALF), (ROWS, HALF), (2 * ROWS, HALF)]
    shapes += [(2 * MEM, HALF)] * 8
    return pl.pallas_call(
        attention_kernel,
        in_specs=[SMEM] + [VMEM] * 9,
        out_specs=[VMEM] * 12,
        out_shape=[jax.ShapeDtypeStruct(shape, LOW) for shape in shapes],
        compiler_params=pltpu.CompilerParams(vmem_limit_bytes=28 << 20),
        cost_estimate=pl.CostEstimate(
            flops=int(8e9), bytes_accessed=5 << 20, transcendentals=2 << 20
        ),
        name="attention_backward",
    )(place, q, g, k, v, far, *memory)


def product_half(place, half, out, refs):
    first, rest, pieces = refs[:4], refs[4:6], refs[6:10]
    left = jnp.concatenate(
        [ref[half] for ref in first] + [rest[0][half]] + [rest[1][k, half] for k in range(3)],
        axis=1,
    )
    for n in range(4):
        cols = slice(n * PAIR, (n + 1) * PAIR)
        right = jnp.concatenate(
            [p[0:ROWS, cols] for p in pieces] + [p[ROWS:, cols] for p in pieces], axis=0
        )
        out[:, cols] = dot(left, right, 1, 0).astype(LOW)


def give_kernel(place, *refs):
    product_half(place, 1 - place[0], refs[17], refs)


def keep_kernel(place, *refs):
    product_half(place, place[0], refs[11], refs)


def product_give(place, sources, carried, after):
    return pl.pallas_call(
        give_kernel,
        in_specs=[SMEM] + [VMEM] * 10 + [ANY] * 7,
        out_specs=[VMEM] + [ANY] * 6,
        out_shape=[jax.ShapeDtypeStruct((512, HALF), LOW)]
        + [jax.ShapeDtypeStruct(a.shape, LOW) for a in carried],
        input_output_aliases={11 + n: 1 + n for n in range(6)},
        compiler_params=pltpu.CompilerParams(vmem_limit_bytes=24 << 20),
        cost_estimate=pl.CostEstimate(flops=int(1e9), bytes_accessed=4 << 20, transcendentals=0),
        name="product_give",
    )(place, *sources, *carried, after)


def product_keep(place, sources, after):
    return pl.pallas_call(
        keep_kernel,
        in_specs=[SMEM] + [VMEM] * 10 + [ANY],
        out_specs=VMEM,
        out_shape=jax.ShapeDtypeStruct((512, HALF), LOW),
        compiler_params=pltpu.CompilerParams(vmem_limit_bytes=24 << 20),
        cost_estimate=pl.CostEstimate(flops=int(2e9), bytes_accessed=4 << 20, transcendentals=0),
        name="product_keep",
    )(place, *sources, after)


def merge_kernel(a_ref, b_ref, out_ref):
    out_ref[...] = (a_ref[...].astype(FULL) + b_ref[...].astype(FULL)).astype(LOW)


def merge(keep, swapped):
    return pl.pallas_call(
        merge_kernel,
        in_specs=[VMEM] * 2,
        out_specs=VMEM,
        out_shape=jax.ShapeDtypeStruct(keep.shape, LOW),
        compiler_params=pltpu.CompilerParams(vmem_limit_bytes=16 << 20),
        cost_estimate=pl.CostEstimate(flops=1 << 20, bytes_accessed=3 << 20, transcendentals=0),
        name="core_sum",
    )(keep, swapped)


def join_kernel(a_ref, b_ref, out_ref):
    out_ref[0] = a_ref[...]
    out_ref[1] = b_ref[...]


def join(a, b):
    return pl.pallas_call(
        join_kernel,
        in_specs=[VMEM] * 2,
        out_specs=VMEM,
        out_shape=jax.ShapeDtypeStruct((2, *a.shape), LOW),
        compiler_params=pltpu.CompilerParams(vmem_limit_bytes=8 << 20),
        cost_estimate=pl.CostEstimate(flops=0, bytes_accessed=1 << 20, transcendentals=0),
        name="join_memory",
    )(a, b)


def stack_kernel(*refs):
    for n in range(3):
        refs[-1][n] = refs[n][...]


def stack(arrays, after):
    return pl.pallas_call(
        stack_kernel,
        in_specs=[VMEM] * 3 + [ANY] * len(after),
        out_specs=VMEM,
        out_shape=jax.ShapeDtypeStruct((3, *arrays[0].shape), LOW),
        compiler_params=pltpu.CompilerParams(vmem_limit_bytes=16 << 20),
        cost_estimate=pl.CostEstimate(flops=0, bytes_accessed=2 << 20, transcendentals=0),
        name="stack_hidden",
    )(*arrays, *after)


def total_of(refs):
    total = refs[0][...].astype(FULL)
    for ref in refs[1:]:
        total = total + ref[...].astype(FULL)
    return total.astype(LOW)


def terms_kernel(*refs):
    refs[4][...] = total_of(refs[:4])


def sum_terms(terms):
    return pl.pallas_call(
        terms_kernel,
        in_specs=[VMEM] * 4,
        out_specs=VMEM,
        out_shape=jax.ShapeDtypeStruct((2 * MEM, HALF), LOW),
        compiler_params=pltpu.CompilerParams(vmem_limit_bytes=16 << 20),
        cost_estimate=pl.CostEstimate(flops=1 << 20, bytes_accessed=2 << 20, transcendentals=0),
        name="memory_sum",
    )(*terms)


def unpack_kernel(place, gq_ref, local_ref, first_ref, back_ref, got_ref, *refs):
    terms, outs = refs[:4], refs[4:]
    mine = pl.ds(pl.multiple_of(place[1] * HALF, HALF), HALF)
    theirs = pl.ds(pl.multiple_of((1 - place[1]) * HALF, HALF), HALF)
    outs[0][:, mine] = gq_ref[0:ROWS, :]
    outs[1][:, mine] = local_ref[0:ROWS, :]
    outs[2][:, mine] = local_ref[ROWS:, :]
    outs[0][:, theirs] = first_ref[...]
    outs[1][:, theirs] = back_ref[0:ROWS, :]
    outs[2][:, theirs] = back_ref[ROWS:, :]
    for value, cols in ((total_of(terms), mine), (got_ref[...], theirs)):
        outs[3][:, cols] = value[0:MEM, :]
        outs[4][:, cols] = value[MEM:, :]


def unpack(place, gq, local_grads, first, back, got, terms):
    return pl.pallas_call(
        unpack_kernel,
        in_specs=[SMEM] + [VMEM] * 9,
        out_specs=[VMEM] * 5,
        out_shape=[jax.ShapeDtypeStruct((ROWS, INNER), LOW)] * 3
        + [jax.ShapeDtypeStruct((MEM, INNER), LOW)] * 2,
        compiler_params=pltpu.CompilerParams(vmem_limit_bytes=16 << 20),
        cost_estimate=pl.CostEstimate(flops=0, bytes_accessed=4 << 20, transcendentals=0),
        name="unpack_heads",
    )(place, gq, local_grads, first, back, got, *terms)


def finish_kernel(in_ref, out_ref):
    for y in range(2):
        total = in_ref[y].astype(FULL)
        for n in range(1, 16):
            total = total + in_ref[2 * n + y].astype(FULL)
        out_ref[:, y * HALF : (y + 1) * HALF] = total * (1.0 / 256)


def finish(along):
    return pl.pallas_call(
        finish_kernel,
        in_specs=[VMEM],
        out_specs=VMEM,
        out_shape=jax.ShapeDtypeStruct((16, INNER), FULL),
        compiler_params=pltpu.CompilerParams(vmem_limit_bytes=16 << 20),
        cost_estimate=pl.CostEstimate(flops=1 << 20, bytes_accessed=1 << 20, transcendentals=0),
        name="weight_sum",
    )(along)


def local(
    hidden_states, queries, local_keys, local_values, memory_keys, memory_values, grad_output
):
    core = lax.rem(lax.axis_index("group"), 2)
    member = lax.axis_index("member")
    place = jnp.stack((core, member // 4, member, lax.rem(member, 4))).astype(jnp.int32)

    own_memory, give_memory = pack_memory(memory_keys, memory_values)
    other_memory = shift(give_memory, "yl", 2, 1)
    give_queries = pack_queries(
        place, queries, grad_output, local_keys, local_values, [own_memory]
    )
    joined = join(own_memory, other_memory)
    memory = [joined] + [shift(joined, "x", 4, k) for k in (1, 2, 3)]
    (give_queries,) = gate([give_queries], [joined])
    far_queries = shift(give_queries, "yl", 2, 1)

    hidden = hidden_pieces(place, hidden_states, [give_queries, joined])
    hidden = gate(hidden, memory[2:])
    near = [hidden[0]] + [shift(hidden[k], "x", 4, k) for k in (1, 2, 3)]

    gq, local_grads, first, back, *terms = attention(
        place, queries, grad_output, local_keys, local_values, far_queries, memory
    )
    pieces = [gq] + [shift(gq, "x", 4, k) for k in (1, 2, 3)]
    far = [shift(near[0], "yl", 2, 1)]
    far.append(shift(stack(near[1:], [gq, far[0]]), "yl", 2, 1))
    back = shift(back, "yl", 2, 1)
    first = shift(first, "yl", 2, 1)
    sources = near + far + pieces
    give, *moving = product_give(place, sources, terms[1:4] + terms[5:], first)
    keep = product_keep(place, sources, give)
    swapped = shift(give, "c", 2, 1)
    both = merge(keep, swapped)
    along = lax.all_to_all(
        both.reshape(32, 16, HALF), AXES, 0, 0, axis_index_groups=ZY_GROUPS, tiled=True
    )
    others = [terms[4]] + [shift(moving[2 + k], "x", 4, 4 - k) for k in (1, 2, 3)]
    got_sum = shift(sum_terms(others), "yl", 2, 1)
    nears = [terms[0]] + [shift(moving[k - 1], "x", 4, 4 - k) for k in (1, 2, 3)]
    gq_out, glk, glv, gmk, gmv = unpack(
        place, gq, local_grads, first, back, got_sum, nears
    )
    grad_weight = finish(along)
    return gq_out, glk, glv, gmk, gmv, grad_weight


def solution(mesh):
    spec = P(("group", "member"), None)
    return jax.shard_map(
        local, mesh=mesh, in_specs=(spec,) * 7, out_specs=(spec,) * 6, check_vma=False
    )
```

```python
import jax
import jax.numpy as jnp
from jax import lax
from jax.experimental import pallas as pl
from jax.experimental.pallas import tpu as pltpu
from jax.sharding import PartitionSpec as P

HEAD_DIM = 128
DOCS = 8
ROWS = 128
MEM = 64
WIDTH = 4096
INNER = 2048
HALF = INNER // 2
PAIR = 2 * HEAD_DIM
AXES = ("group", "member")
LOW = jnp.bfloat16
FULL = jnp.float32


def coords(i):
    g, m = divmod(i, 8)
    return {"z": g // 4, "yh": (g // 2) % 2, "c": g % 2, "yl": m // 4, "x": m % 4}


def index_of(d):
    return (d["z"] * 4 + d["yh"] * 2 + d["c"]) * 8 + d["yl"] * 4 + d["x"]


def pairs(key, size, step):
    out = []
    for i in range(256):
        d = coords(i)
        d[key] = (d[key] + step) % size
        out.append((i, index_of(d)))
    return out


ZY_GROUPS = [
    [
        index_of({"z": z, "yh": yh, "c": c, "yl": yl, "x": x})
        for z in range(8)
        for yh in range(2)
        for yl in range(2)
    ]
    for c in range(2)
    for x in range(4)
]
ANY = pl.BlockSpec(memory_space=pl.ANY)
VMEM = pl.BlockSpec(memory_space=pltpu.VMEM)
SMEM = pl.BlockSpec(memory_space=pltpu.SMEM)


def shift(array, key, size, step):
    return lax.ppermute(array, AXES, pairs(key, size, step))


def dot(left, right, left_dim, right_dim):
    return lax.dot_general(
        left, right, (((left_dim,), (right_dim,)), ((), ())), preferred_element_type=FULL
    )


def pack_memory_kernel(mk_ref, mv_ref, near_ref, far_ref):
    yl = lax.axis_index("member") // 4
    for out, half in ((near_ref, yl), (far_ref, 1 - yl)):
        cols = pl.ds(pl.multiple_of(half * HALF, HALF), HALF)
        out[0:MEM, :] = mk_ref[:, cols]
        out[MEM:, :] = mv_ref[:, cols]


def pack_memory(mk, mv):
    return pl.pallas_call(
        pack_memory_kernel,
        in_specs=[VMEM, VMEM],
        out_specs=[VMEM] * 2,
        out_shape=[jax.ShapeDtypeStruct((2 * MEM, HALF), LOW)] * 2,
        cost_estimate=pl.CostEstimate(flops=0, bytes_accessed=1 << 20, transcendentals=0),
        name="pack_memory",
    )(mk, mv)


def pack_queries_kernel(place, q_ref, g_ref, k_ref, v_ref, *rest):
    out = rest[-1]
    for n, ref in enumerate((q_ref, g_ref, k_ref, v_ref)):
        out[n * ROWS : (n + 1) * ROWS, :] = ref[...]


def pack_queries(place, q, g, k, v, after):
    tall = pl.BlockSpec((ROWS, HALF), lambda i, s: (0, 1 - s[1]))
    return pl.pallas_call(
        pack_queries_kernel,
        grid_spec=pltpu.PrefetchScalarGridSpec(
            num_scalar_prefetch=1,
            grid=(1,),
            in_specs=[tall] * 4 + [ANY] * len(after),
            out_specs=pl.BlockSpec((4 * ROWS, HALF), lambda i, s: (0, 0)),
        ),
        out_shape=jax.ShapeDtypeStruct((4 * ROWS, HALF), LOW),
        cost_estimate=pl.CostEstimate(flops=0, bytes_accessed=2 << 20, transcendentals=0),
        name="pack_queries",
    )(place, q, g, k, v, *after)


def hidden_kernel(place, h_ref, *refs):
    outs, perm = refs[-5:-1], refs[-1]
    dst = lax.broadcasted_iota(jnp.int32, (1024, 1), 0)
    src = lax.broadcasted_iota(jnp.int32, (1024, 1024), 1)
    x, c, zl = ((dst >> 8) + place[3]) & 3, (dst >> 7) & 1, (dst >> 6) & 1
    yh, yl, i = (dst >> 5) & 1, (dst >> 4) & 1, dst & 15
    want = (zl << 9) | (yh << 8) | (c << 7) | (yl << 6) | (x << 4) | i
    perm[...] = jnp.where(src == want, 1.0, 0.0).astype(LOW)
    for t in range(4):
        moved = dot(perm[...], h_ref[:, t * 1024 : (t + 1) * 1024], 1, 1).astype(LOW)
        for k, out in enumerate(outs):
            for c in range(2):
                row = k * 256 + c * 128
                out[c, t * 128 : (t + 1) * 128, :] = moved[row : row + 128, :]


def hidden_pieces(place, hidden, after):
    return pl.pallas_call(
        hidden_kernel,
        in_specs=[SMEM, VMEM] + [ANY] * len(after),
        out_specs=[VMEM] * 4,
        out_shape=[jax.ShapeDtypeStruct((2, 512, ROWS), LOW)] * 4,
        scratch_shapes=[pltpu.VMEM((1024, 1024), LOW)],
        compiler_params=pltpu.CompilerParams(vmem_limit_bytes=24 << 20),
        cost_estimate=pl.CostEstimate(flops=1 << 30, bytes_accessed=2 << 20, transcendentals=0),
        name="pack_hidden",
    )(place, hidden, *after)


def gate_kernel(*refs):
    pass


def gate(arrays, after):
    count = len(arrays)
    return pl.pallas_call(
        gate_kernel,
        in_specs=[ANY] * (count + len(after)),
        out_specs=[ANY] * count,
        out_shape=[jax.ShapeDtypeStruct(a.shape, a.dtype) for a in arrays],
        input_output_aliases={n: n for n in range(count)},
        compiler_params=pltpu.CompilerParams(vmem_limit_bytes=1 << 20),
        name="gate",
    )(*arrays, *after)


def attention_kernel(place, q_ref, g_ref, k_ref, v_ref, far_ref, *refs):
    memory = refs[:4]
    gq_ref, local_ref, first_ref, back_ref = refs[4:8]
    term_refs = refs[8:]
    scale = HEAD_DIM**-0.5
    key_at = lax.broadcasted_iota(jnp.int32, (ROWS, ROWS), 0)
    query_at = lax.broadcasted_iota(jnp.int32, (ROWS, ROWS), 1)
    visible = key_at <= query_at
    def one_head(head):
        cols = pl.ds(pl.multiple_of(head * HEAD_DIM, HEAD_DIM), HEAD_DIM)
        mine_cols = pl.ds(pl.multiple_of(place[1] * HALF + head * HEAD_DIM, HEAD_DIM), HEAD_DIM)
        q, g, k, v = [
            [ref[:, mine_cols], far_ref[n * ROWS : (n + 1) * ROWS, cols]]
            for n, ref in enumerate((q_ref, g_ref, k_ref, v_ref))
        ]
        mk = jnp.concatenate([ref[n, 0:MEM, cols] for n in range(2) for ref in memory], axis=0)
        mv = jnp.concatenate([ref[n, MEM:, cols] for n in range(2) for ref in memory], axis=0)
        both_q = jnp.concatenate(q, axis=0)
        both_g = jnp.concatenate(g, axis=0)
        s_loc = jnp.concatenate(
            [jnp.where(visible, dot(k[n], q[n], 1, 1) * scale, -jnp.inf) for n in range(2)],
            axis=1,
        )
        dp_loc = jnp.concatenate([dot(v[n], g[n], 1, 1) for n in range(2)], axis=1)
        s_mem = dot(mk, both_q, 1, 1) * scale
        dp_mem = dot(mv, both_g, 1, 1)
        top = jnp.maximum(
            jnp.max(s_loc, axis=0, keepdims=True), jnp.max(s_mem, axis=0, keepdims=True)
        )
        e_loc = jnp.exp(s_loc - top)
        e_mem = jnp.exp(s_mem - top)
        total = jnp.sum(e_loc, axis=0, keepdims=True) + jnp.sum(e_mem, axis=0, keepdims=True)
        inverse = 1.0 / total
        p_loc = e_loc * inverse
        p_mem = e_mem * inverse
        delta = jnp.sum(p_loc * dp_loc, axis=0, keepdims=True) + jnp.sum(
            p_mem * dp_mem, axis=0, keepdims=True
        )
        ds_loc = (p_loc * (dp_loc - delta)).astype(LOW)
        ds_mem = (p_mem * (dp_mem - delta)).astype(LOW)
        low_loc = p_loc.astype(LOW)
        gq_mem = dot(ds_mem, mk, 0, 0)
        gq, glk, glv = [], [], []
        for n in range(2):
            rows = slice(n * ROWS, (n + 1) * ROWS)
            mine = ds_loc[:, rows]
            gq.append((scale * (dot(mine, k[n], 0, 0) + gq_mem[rows, :])).astype(LOW))
            glk.append((scale * dot(mine, q[n], 1, 0)).astype(LOW))
            glv.append(dot(low_loc[:, rows], g[n], 1, 0).astype(LOW))
        gq_ref[0:ROWS, cols] = gq[0]
        gq_ref[ROWS:, cols] = gq[1]
        local_ref[0:ROWS, cols] = glk[0]
        local_ref[ROWS:, cols] = glv[0]
        first_ref[:, cols] = gq[1]
        back_ref[0:ROWS, cols] = glk[1]
        back_ref[ROWS:, cols] = glv[1]
        dk = (scale * dot(ds_mem, both_q, 1, 0)).astype(LOW)
        dv = dot(p_mem.astype(LOW), both_g, 1, 0).astype(LOW)
        for n in range(8):
            rows = slice(n * MEM, (n + 1) * MEM)
            term_refs[n][0:MEM, cols] = dk[rows, :]
            term_refs[n][MEM:, cols] = dv[rows, :]

    def four_heads(step, carry):
        for n in range(4):
            one_head(4 * step + n)
        return carry

    lax.fori_loop(0, 2, four_heads, 0)


def attention(place, q, g, k, v, far, memory):
    shapes = [(2 * ROWS, HALF), (2 * ROWS, HALF), (ROWS, HALF), (2 * ROWS, HALF)]
    shapes += [(2 * MEM, HALF)] * 8
    return pl.pallas_call(
        attention_kernel,
        in_specs=[SMEM] + [VMEM] * 9,
        out_specs=[VMEM] * 12,
        out_shape=[jax.ShapeDtypeStruct(shape, LOW) for shape in shapes],
        compiler_params=pltpu.CompilerParams(vmem_limit_bytes=28 << 20),
        cost_estimate=pl.CostEstimate(
            flops=int(8e9), bytes_accessed=5 << 20, transcendentals=2 << 20
        ),
        name="attention_backward",
    )(place, q, g, k, v, far, *memory)


def product_half(place, half, out, refs):
    first, rest, pieces = refs[:4], refs[4:6], refs[6:10]
    left = jnp.concatenate(
        [ref[half] for ref in first] + [rest[0][half]] + [rest[1][k, half] for k in range(3)],
        axis=1,
    )
    for n in range(4):
        cols = slice(n * PAIR, (n + 1) * PAIR)
        right = jnp.concatenate(
            [p[0:ROWS, cols] for p in pieces] + [p[ROWS:, cols] for p in pieces], axis=0
        )
        out[:, cols] = dot(left, right, 1, 0).astype(LOW)


def give_kernel(place, *refs):
    product_half(place, 1 - place[0], refs[17], refs)


def keep_kernel(place, *refs):
    product_half(place, place[0], refs[11], refs)


def product_give(place, sources, carried, after):
    return pl.pallas_call(
        give_kernel,
        in_specs=[SMEM] + [VMEM] * 10 + [ANY] * 7,
        out_specs=[VMEM] + [ANY] * 6,
        out_shape=[jax.ShapeDtypeStruct((512, HALF), LOW)]
        + [jax.ShapeDtypeStruct(a.shape, LOW) for a in carried],
        input_output_aliases={11 + n: 1 + n for n in range(6)},
        compiler_params=pltpu.CompilerParams(vmem_limit_bytes=24 << 20),
        cost_estimate=pl.CostEstimate(flops=int(1e9), bytes_accessed=4 << 20, transcendentals=0),
        name="product_give",
    )(place, *sources, *carried, after)


def product_keep(place, sources, after):
    return pl.pallas_call(
        keep_kernel,
        in_specs=[SMEM] + [VMEM] * 10 + [ANY],
        out_specs=VMEM,
        out_shape=jax.ShapeDtypeStruct((512, HALF), LOW),
        compiler_params=pltpu.CompilerParams(vmem_limit_bytes=24 << 20),
        cost_estimate=pl.CostEstimate(flops=int(2e9), bytes_accessed=4 << 20, transcendentals=0),
        name="product_keep",
    )(place, *sources, after)


def merge_kernel(a_ref, b_ref, out_ref):
    out_ref[...] = (a_ref[...].astype(FULL) + b_ref[...].astype(FULL)).astype(LOW)


def merge(keep, swapped):
    return pl.pallas_call(
        merge_kernel,
        in_specs=[VMEM] * 2,
        out_specs=VMEM,
        out_shape=jax.ShapeDtypeStruct(keep.shape, LOW),
        compiler_params=pltpu.CompilerParams(vmem_limit_bytes=16 << 20),
        cost_estimate=pl.CostEstimate(flops=1 << 20, bytes_accessed=3 << 20, transcendentals=0),
        name="core_sum",
    )(keep, swapped)


def join_kernel(a_ref, b_ref, out_ref):
    out_ref[0] = a_ref[...]
    out_ref[1] = b_ref[...]


def join(a, b):
    return pl.pallas_call(
        join_kernel,
        in_specs=[VMEM] * 2,
        out_specs=VMEM,
        out_shape=jax.ShapeDtypeStruct((2, *a.shape), LOW),
        compiler_params=pltpu.CompilerParams(vmem_limit_bytes=8 << 20),
        cost_estimate=pl.CostEstimate(flops=0, bytes_accessed=1 << 20, transcendentals=0),
        name="join_memory",
    )(a, b)


def stack_kernel(*refs):
    for n in range(3):
        refs[-1][n] = refs[n][...]


def stack(arrays, after):
    return pl.pallas_call(
        stack_kernel,
        in_specs=[VMEM] * 3 + [ANY] * len(after),
        out_specs=VMEM,
        out_shape=jax.ShapeDtypeStruct((3, *arrays[0].shape), LOW),
        compiler_params=pltpu.CompilerParams(vmem_limit_bytes=16 << 20),
        cost_estimate=pl.CostEstimate(flops=0, bytes_accessed=2 << 20, transcendentals=0),
        name="stack_hidden",
    )(*arrays, *after)


def total_of(refs):
    total = refs[0][...].astype(FULL)
    for ref in refs[1:]:
        total = total + ref[...].astype(FULL)
    return total.astype(LOW)


def terms_kernel(*refs):
    refs[4][...] = total_of(refs[:4])


def sum_terms(terms):
    return pl.pallas_call(
        terms_kernel,
        in_specs=[VMEM] * 4,
        out_specs=VMEM,
        out_shape=jax.ShapeDtypeStruct((2 * MEM, HALF), LOW),
        compiler_params=pltpu.CompilerParams(vmem_limit_bytes=16 << 20),
        cost_estimate=pl.CostEstimate(flops=1 << 20, bytes_accessed=2 << 20, transcendentals=0),
        name="memory_sum",
    )(*terms)


def unpack_kernel(place, gq_ref, local_ref, first_ref, back_ref, got_ref, *refs):
    terms, outs = refs[:4], refs[4:]
    mine = pl.ds(pl.multiple_of(place[1] * HALF, HALF), HALF)
    theirs = pl.ds(pl.multiple_of((1 - place[1]) * HALF, HALF), HALF)
    outs[0][:, mine] = gq_ref[0:ROWS, :]
    outs[1][:, mine] = local_ref[0:ROWS, :]
    outs[2][:, mine] = local_ref[ROWS:, :]
    outs[0][:, theirs] = first_ref[...]
    outs[1][:, theirs] = back_ref[0:ROWS, :]
    outs[2][:, theirs] = back_ref[ROWS:, :]
    for value, cols in ((total_of(terms), mine), (got_ref[...], theirs)):
        outs[3][:, cols] = value[0:MEM, :]
        outs[4][:, cols] = value[MEM:, :]


def unpack(place, gq, local_grads, first, back, got, terms):
    return pl.pallas_call(
        unpack_kernel,
        in_specs=[SMEM] + [VMEM] * 9,
        out_specs=[VMEM] * 5,
        out_shape=[jax.ShapeDtypeStruct((ROWS, INNER), LOW)] * 3
        + [jax.ShapeDtypeStruct((MEM, INNER), LOW)] * 2,
        compiler_params=pltpu.CompilerParams(vmem_limit_bytes=16 << 20),
        cost_estimate=pl.CostEstimate(flops=0, bytes_accessed=4 << 20, transcendentals=0),
        name="unpack_heads",
    )(place, gq, local_grads, first, back, got, *terms)


def finish_kernel(in_ref, out_ref):
    for y in range(2):
        total = in_ref[y].astype(FULL)
        for n in range(1, 16):
            total = total + in_ref[2 * n + y].astype(FULL)
        out_ref[:, y * HALF : (y + 1) * HALF] = total * (1.0 / 256)


def finish(along):
    return pl.pallas_call(
        finish_kernel,
        in_specs=[VMEM],
        out_specs=VMEM,
        out_shape=jax.ShapeDtypeStruct((16, INNER), FULL),
        compiler_params=pltpu.CompilerParams(vmem_limit_bytes=16 << 20),
        cost_estimate=pl.CostEstimate(flops=1 << 20, bytes_accessed=1 << 20, transcendentals=0),
        name="weight_sum",
    )(along)


def local(
    hidden_states, queries, local_keys, local_values, memory_keys, memory_values, grad_output
):
    core = lax.rem(lax.axis_index("group"), 2)
    member = lax.axis_index("member")
    place = jnp.stack((core, member // 4, member, lax.rem(member, 4))).astype(jnp.int32)

    own_memory, give_memory = pack_memory(memory_keys, memory_values)
    other_memory = shift(give_memory, "yl", 2, 1)
    give_queries = pack_queries(
        place, queries, grad_output, local_keys, local_values, [own_memory]
    )
    joined = join(own_memory, other_memory)
    memory = [joined] + [shift(joined, "x", 4, k) for k in (1, 2, 3)]
    (give_queries,) = gate([give_queries], [joined])
    far_queries = shift(give_queries, "yl", 2, 1)

    hidden = hidden_pieces(place, hidden_states, [give_queries, joined])
    hidden = gate(hidden, memory[2:])
    near = [hidden[0]] + [shift(hidden[k], "x", 4, k) for k in (1, 2, 3)]

    gq, local_grads, first, back, *terms = attention(
        place, queries, grad_output, local_keys, local_values, far_queries, memory
    )
    pieces = [gq] + [shift(gq, "x", 4, k) for k in (1, 2, 3)]
    far = [shift(near[0], "yl", 2, 1)]
    far.append(shift(stack(near[1:], [gq, far[0]]), "yl", 2, 1))
    back = shift(back, "yl", 2, 1)
    first = shift(first, "yl", 2, 1)
    sources = near + far + pieces
    give, *moving = product_give(place, sources, terms[1:4] + terms[5:], first)
    keep = product_keep(place, sources, give)
    swapped = shift(give, "c", 2, 1)
    both = merge(keep, swapped)
    along = lax.all_to_all(
        both.reshape(32, 16, HALF), AXES, 0, 0, axis_index_groups=ZY_GROUPS, tiled=True
    )
    others = [terms[4]] + [shift(moving[2 + k], "x", 4, 4 - k) for k in (1, 2, 3)]
    got_sum = shift(sum_terms(others), "yl", 2, 1)
    nears = [terms[0]] + [shift(moving[k - 1], "x", 4, 4 - k) for k in (1, 2, 3)]
    gq_out, glk, glv, gmk, gmv = unpack(
        place, gq, local_grads, first, back, got_sum, nears
    )
    grad_weight = finish(along)
    return gq_out, glk, glv, gmk, gmv, grad_weight


def solution(mesh):
    spec = P(("group", "member"), None)
    return jax.shard_map(
        local, mesh=mesh, in_specs=(spec,) * 7, out_specs=(spec,) * 6, check_vma=False
    )
```
